32 devices in a mesh: dp: 16 (over z, y, x), mp: 2 (over core).
Axes of the slice: x: 2, y: 2, z: 4, core: 2. Of those that a mesh axis runs over, the one named last changes fastest.
Arguments:
- x_in: bfloat16 [4096, 2048], P('dp'), may hold values from -6 to 6
- cotangent: bfloat16 [4096, 7168], P('dp', 'mp'), may hold values from -6 to 6
- w_gate: bfloat16 [2048, 7168], P('dp', 'mp'), may hold values from -0.125 to 0.125
- w_up: bfloat16 [2048, 7168], P('dp', 'mp'), may hold values from -0.125 to 0.125
- send_counts: int32 [16, 16], P('dp'), may hold values from 0 to 4, as said below
- recv_counts: int32 [16, 16], P('dp'), may hold values from 0 to 4, as said below
Outputs:
- grad_x: bfloat16 [4096, 2048], P('dp', 'mp')
- grad_gate: float32 [2048, 7168], P('dp', 'mp')
The draws below stay inside these ranges and needn't reach their ends.
Inputs may be any that keep to these rules, and one draw needn't show every extreme that they name: `send_counts`: each entry is 0 to 4. A quarter of the indices only send and the rest only receive; one sending index sends 4 rows to every receiver, so its live rows reach 256. recv_counts is the transpose of send_counts.
All inputs are finite; a program needn't handle non-finite values.
Results may differ from the reference program's by a relative error of at most 0.014.
Values may be sent and summed in bfloat16 or wider, within the bound.
No kernel may reach another device: no remote copies, remote signals or barrier semaphores. Data moves between devices by JAX's collectives and lax.ppermute only.
A program may use at most 192 MiB of HBM per device.

```python
import jax
import jax.numpy as jnp
from jax import lax

D = 2048
FF = 7168
BAL = 208
SLOT = 4
CAP = 256
ROWS = 4096
N_DP = 16
N_MP = 2


def plan_counts(key):
    order = jax.random.permutation(jax.random.fold_in(key, 11), N_DP)
    heavy = order < N_DP // 4
    spread = jax.random.randint(jax.random.fold_in(key, 12), (N_DP, N_DP), 0, SLOT + 1)
    spread = jnp.where((order == 0)[:, None], SLOT, spread)
    pairs = heavy[:, None] & jnp.logical_not(heavy)[None, :]
    return jnp.where(pairs, spread, 0).astype(jnp.int32)


def draw_send_counts(key, part):
    return plan_counts(key)


def draw_recv_counts(key, part):
    return plan_counts(key).T


def steps_of(key, extent, cuts, low, high):
    def one(dim, blocks):
        heights = jax.random.uniform(jax.random.fold_in(jax.random.fold_in(key, 6), dim), (blocks,), jnp.float32, low / len(cuts), high / len(cuts))
        return jnp.repeat(jnp.exp(heights), extent[dim] // blocks).reshape((-1,) + (1,) * (len(extent) - dim - 1))

    gain = one(*cuts[0])
    for cut in cuts[1:]:
        gain = gain * one(*cut)
    return gain


def bell_draw(rng, dims, deviation, limit, split=(), kind=jnp.bfloat16):
    gain = steps_of(rng, dims, split, -0.22, 0.18) if split else 1.0
    result = jax.random.normal(rng, dims, jnp.float32) * deviation * gain
    return jnp.minimum(jnp.maximum(result, -limit), limit).astype(kind)


def setup_inputs(seed: int = 0) -> dict:
    streams_of = jax.random.split(jax.random.key(seed), 7)
    x_in = bell_draw(streams_of[0], (ROWS, D), 1.0, 6.0, ((0, 16),))
    cotangent = bell_draw(streams_of[1], (ROWS, FF), 1.0, 6.0, ((0, 16), (1, 2)))
    w_gate = bell_draw(streams_of[2], (D, FF), D ** -0.5, 0.125, ((0, 16), (1, 2)))
    w_up = bell_draw(streams_of[3], (D, FF), D ** -0.5, 0.125, ((0, 16), (1, 2)))
    send_counts = draw_send_counts(jax.random.fold_in(streams_of[6], 71), 0)
    recv_counts = draw_recv_counts(jax.random.fold_in(streams_of[6], 71), 0)
    return dict(x_in=x_in, cotangent=cotangent, w_gate=w_gate, w_up=w_up, send_counts=send_counts, recv_counts=recv_counts)


def reference(x_in, cotangent, w_gate, w_up, send_counts, recv_counts):
    sent_total = jnp.sum(send_counts, axis=1).astype(jnp.int32)
    got_total = jnp.sum(recv_counts, axis=1).astype(jnp.int32)
    live = (BAL + sent_total - got_total).astype(jnp.int32)
    live_end = jnp.cumsum(live).astype(jnp.int32)
    live_start = (live_end - live).astype(jnp.int32)
    position = jnp.arange(N_DP * BAL, dtype=jnp.int32)
    owner = jnp.sum((live_end[None, :] <= position[:, None]).astype(jnp.int32), axis=1).astype(jnp.int32)
    row_index = (owner * CAP + position - live_start[owner]).astype(jnp.int32)
    x_rows = x_in[row_index]
    cot_rows = cotangent[row_index]
    hidden_group = FF // N_MP
    gate_three = w_gate.astype(jnp.float32).reshape(D, N_MP, hidden_group)
    up_three = w_up.astype(jnp.float32).reshape(D, N_MP, hidden_group)

    def step(grad_total, block):
        x_block, cot_block = block
        gate_val = jnp.dot(x_block, w_gate, preferred_element_type=jnp.float32)
        up_val = jnp.dot(x_block, w_up, preferred_element_type=jnp.float32)
        sig = jax.nn.sigmoid(gate_val)
        cot_val = cot_block.astype(jnp.float32)
        d_gate = (cot_val * up_val * sig * (1.0 + gate_val * (1.0 - sig))).astype(jnp.bfloat16)
        d_up = (cot_val * gate_val * sig).astype(jnp.bfloat16)
        partial_value = jnp.einsum("rmf,dmf->rmd", d_gate.astype(jnp.float32).reshape(BAL, N_MP, hidden_group), gate_three)
        partial_value = partial_value + jnp.einsum("rmf,dmf->rmd", d_up.astype(jnp.float32).reshape(BAL, N_MP, hidden_group), up_three)
        rounded = lax.optimization_barrier(partial_value.astype(jnp.bfloat16))
        grad_rows = jnp.sum(rounded.astype(jnp.float32), axis=1).astype(jnp.bfloat16)
        grad_total = grad_total + lax.dot_general(x_block, d_gate, (((0,), (0,)), ((), ())), preferred_element_type=jnp.float32)
        return grad_total, grad_rows

    start = jnp.zeros((D, FF), jnp.float32)
    grad_gate, grad_rows = lax.scan(step, start, (x_rows.reshape(N_DP, BAL, D), cot_rows.reshape(N_DP, BAL, FF)))
    grad_x = jnp.zeros((N_DP * CAP, D), jnp.bfloat16).at[row_index].set(grad_rows.reshape(N_DP * BAL, D))
    return grad_x, grad_gate
```

```python
import jax
import jax.numpy as jnp
from jax import lax
from jax.experimental import pallas as pl
from jax.experimental.pallas import tpu as pltpu
from jax.sharding import PartitionSpec as P

BAL = 208
BF = jnp.bfloat16
F32 = jnp.float32


def contract_last(left, right):
    return lax.dot_general(
        left, right, (((1,), (1,)), ((), ())), preferred_element_type=F32
    )


def contract_first(left, right):
    return lax.dot_general(
        left, right, (((0,), (0,)), ((), ())), preferred_element_type=F32
    )


def swiglu_back(x_rows, cot_rows, gate_full, up_full, live_mask):
    gate_val = jnp.dot(x_rows, gate_full, preferred_element_type=F32)
    up_val = jnp.dot(x_rows, up_full, preferred_element_type=F32)
    sig = jax.nn.sigmoid(gate_val)
    cot_val = cot_rows.astype(F32)
    d_gate = jnp.where(
        live_mask[:, None], cot_val * up_val * sig * (1.0 + gate_val * (1.0 - sig)), 0.0
    ).astype(BF)
    d_up = jnp.where(live_mask[:, None], cot_val * gate_val * sig, 0.0).astype(BF)
    return contract_last(d_gate, gate_full) + contract_last(d_up, up_full), d_gate


def live_rows_of(send_counts, recv_counts):
    return BAL + jnp.sum(send_counts[0]) - jnp.sum(recv_counts[0])


def general_plan(x_in, cotangent, w_gate, w_up, send_counts, recv_counts):
    dev_count = lax.axis_size("dp")
    gate_full = lax.all_gather(w_gate, "dp", axis=0, tiled=True)
    up_full = lax.all_gather(w_up, "dp", axis=0, tiled=True)
    live_mask = jnp.arange(x_in.shape[0]) < live_rows_of(send_counts, recv_counts)
    partial_value, d_gate = swiglu_back(x_in, cotangent, gate_full, up_full, live_mask)
    grad_x = lax.psum_scatter(
        partial_value.astype(BF), "mp", scatter_dimension=1, tiled=True
    )
    whole = contract_first(x_in, d_gate)
    pieces = lax.all_to_all(
        whole.reshape(dev_count, x_in.shape[1] // dev_count, whole.shape[1]),
        "dp",
        split_axis=0,
        concat_axis=0,
        tiled=True,
    )
    return grad_x, jnp.sum(pieces, axis=0)


PLANES = 4
PLACES = 4


def chunk_kernel(order, x_ref, cot_ref, *refs, offset, first, last):
    width = cot_ref.shape[1]
    blocks = refs[:PLANES]
    refs = refs[PLANES:]
    if not first:
        prev, refs = refs[0], refs[1:]
    gx_ref, refs = refs[0], refs[1:]
    gg_refs, acc = refs[:PLANES], refs[PLANES]
    step = pl.program_id(0)
    ck = blocks[0].shape[1] // 2
    deep = blocks[0].shape[0]
    cot = cot_ref[:, offset : offset + ck].astype(F32)
    both = None
    xs = []
    for r in range(PLANES):
        plane = order[r]
        start = pl.multiple_of((plane % 2) * deep, deep)
        xr = x_ref[plane // 2, :, pl.ds(start, deep)]
        xs.append(xr)
        term = jnp.dot(xr, blocks[r][...], preferred_element_type=F32)
        both = term if both is None else both + term
    gate, up = both[:, :ck], both[:, ck:]
    sig = jax.nn.sigmoid(gate)
    d_gate = (cot * up * sig * (1.0 + gate * (1.0 - sig))).astype(BF)
    d_up = (cot * gate * sig).astype(BF)
    d_both = jnp.concatenate([d_gate, d_up], axis=1)
    for r in range(PLANES):
        plane = order[r]
        start = pl.multiple_of((plane % 2) * deep, deep)
        gx = contract_last(d_both, blocks[r][...])
        spot = (plane // 2, slice(None), pl.ds(start, deep))
        if not first:
            gx = gx + prev[spot].astype(F32)
        gx_ref[spot] = gx.astype(gx_ref.dtype)
        gg = contract_first(xs[r], d_gate)

        @pl.when(step == 0)
        def _():
            acc[r] = gg

        @pl.when(step > 0)
        def _():
            acc[r] += gg

    @pl.when(step == pl.num_programs(0) - 1)
    def _():
        for r in range(PLANES):
            gg_refs[r][...] = acc[r].astype(BF)


def chunk_call(order, x_all, cot_all, blocks, prev, offset, last):
    rows = x_all.shape[1]
    half = x_all.shape[2]
    deep, wide = blocks[0].shape
    ck = wide // 2
    tile = 256
    first = prev is None
    x_spec = pl.BlockSpec((2, tile, half), lambda i, o: (0, i, 0))
    cot_spec = pl.BlockSpec((tile, cot_all.shape[1]), lambda i, o: (i, 0))
    whole = pl.BlockSpec((deep, wide), lambda i, o: (0, 0))
    gg_spec = pl.BlockSpec((deep, ck), lambda i, o: (0, 0))
    outs = pl.pallas_call(
        lambda *a: chunk_kernel(*a, offset=offset, first=first, last=last),
        grid_spec=pltpu.PrefetchScalarGridSpec(
            num_scalar_prefetch=1,
            grid=(rows // tile,),
            in_specs=[x_spec, cot_spec] + [whole] * PLANES + ([] if first else [x_spec]),
            out_specs=[x_spec] + [gg_spec] * PLANES,
            scratch_shapes=[pltpu.VMEM((PLANES, deep, ck), F32)],
        ),
        out_shape=[jax.ShapeDtypeStruct((2, rows, half), BF if last else F32)]
        + [jax.ShapeDtypeStruct((deep, ck), BF)] * PLANES,
        compiler_params=pltpu.CompilerParams(vmem_limit_bytes=40 * 1024 * 1024),
        cost_estimate=pl.CostEstimate(
            flops=10 * rows * 2 * half * ck, bytes_accessed=2**24, transcendentals=rows * ck
        ),
        name="swiglu_chunk",
    )(order, x_all, cot_all, *blocks, *([] if first else [prev]))
    return outs[0], outs[1:]


def at(z, q):
    return z * PLACES + q


def pairs_in_plane(s):
    return [(at(z, q), at(z, q ^ s)) for z in range(PLANES) for q in range(PLACES)]


def pairs_of_planes(moves):
    return [(at(a, q), at(b, q)) for a, b in moves for q in range(PLACES)]


OUTER = pairs_of_planes([(0, 1), (1, 0), (2, 3), (3, 2)])
INNER = pairs_of_planes([(1, 2), (2, 1)])
TO_ENDS = pairs_of_planes([(1, 0), (2, 3)])
FROM_ENDS = pairs_of_planes([(0, 1), (3, 2)])
PLANE_GROUPS = [[at(z, q) for q in range(PLACES)] for z in range(PLANES)]


def send(value, pairs):
    return lax.ppermute(value, "dp", pairs)


def across_plane(value):
    return lax.all_to_all(
        value, "dp", split_axis=0, concat_axis=0, tiled=True, axis_index_groups=PLANE_GROUPS
    )


def gather_planes(own):
    a1 = send(own, OUTER)
    b1 = send(own, INNER)
    a2 = send(a1, INNER)
    b2 = send(b1, TO_ENDS)
    a3 = send(a2, TO_ENDS)
    return own, a1, b1 + b2, a2 + a3


def plane_order(z):
    low = z < 2
    return jnp.stack(
        [z, z ^ 1, jnp.where(low, 2, 1), jnp.where(low, 3, 0)]
    ).astype(jnp.int32)


def add(*terms):
    total = terms[0].astype(F32)
    for term in terms[1:]:
        total = total + term.astype(F32)
    return total.astype(BF)


def sum_planes(parts):
    own, p1, p2, p3 = parts
    r1 = send(p3, FROM_ENDS)
    r2b = send(p2, FROM_ENDS)
    r2a = send(add(p3, r1), INNER)
    r3b = send(add(p2, r2b), INNER)
    r3a = send(add(p1, r2a), OUTER)
    return add(own, r3a, r3b)


def planes_plan(x_in, cotangent, w_gate, w_up, send_counts, recv_counts):
    rows, width = x_in.shape
    depth, hidden = w_gate.shape
    quarter = hidden // PLACES
    half = width // 2
    core = lax.axis_index("mp")
    index = lax.axis_index("dp")
    z = index // PLACES
    chunks = [256, 384, 256] if quarter == 896 else [quarter]
    swap = [(0, 1), (1, 0)]

    gate_q = w_gate.reshape(depth, PLACES, quarter)
    up_q = w_up.reshape(depth, PLACES, quarter)
    blocks = []
    offset = 0
    for ck in chunks:
        part = jnp.concatenate(
            [gate_q[:, :, offset : offset + ck], up_q[:, :, offset : offset + ck]], axis=2
        )
        own = across_plane(part.transpose(1, 0, 2)).reshape(PLACES * depth, 2 * ck)
        blocks.append(gather_planes(own))
        offset += ck

    x_half = lax.dynamic_slice_in_dim(x_in, core * half, half, 1)
    mine = jnp.concatenate(
        [x_half] + [send(x_half, pairs_in_plane(s)) for s in range(1, PLACES)], axis=0
    )
    other = lax.ppermute(mine, "mp", swap)
    x_all = jnp.where(core == 0, jnp.stack([mine, other]), jnp.stack([other, mine]))

    live = jnp.arange(rows) < live_rows_of(send_counts, recv_counts)
    cot_q = jnp.where(live[:, None], cotangent, jnp.zeros((), BF)).reshape(rows, PLACES, quarter)
    place = index % PLACES
    cot_all = jnp.concatenate(
        [
            send(c, pairs_in_plane(s)) if s else c
            for s in range(PLACES)
            for c in [lax.dynamic_index_in_dim(cot_q, place ^ s, 1, keepdims=False)]
        ],
        axis=0,
    )

    order = plane_order(z)
    grads = []
    gx = None
    offset = 0
    for k, ck in enumerate(chunks):
        gx, parts = chunk_call(
            order, x_all, cot_all, blocks[k], gx, offset, k == len(chunks) - 1
        )
        own = sum_planes(parts)
        grads.append(across_plane(own.reshape(PLACES, depth, ck)))
        offset += ck
    grad_gate = (
        jnp.concatenate(grads, axis=2).transpose(1, 0, 2).reshape(depth, hidden).astype(F32)
    )

    theirs = lax.ppermute(lax.dynamic_index_in_dim(gx, 1 - core, 0, keepdims=False), "mp", swap)
    ours = add(lax.dynamic_index_in_dim(gx, core, 0, keepdims=False), theirs)
    ours = ours.reshape(PLACES, rows, half)
    grad_x = add(ours[0], *[send(ours[s], pairs_in_plane(s)) for s in range(1, PLACES)])
    return grad_x, grad_gate


def solution(mesh):
    sizes = dict(mesh.shape)
    by_planes = sizes["dp"] == PLANES * PLACES and sizes["mp"] == 2
    return jax.shard_map(
        planes_plan if by_planes else general_plan,
        mesh=mesh,
        in_specs=(
            P("dp", None),
            P("dp", "mp"),
            P("dp", "mp"),
            P("dp", "mp"),
            P("dp", None),
            P("dp", None),
        ),
        out_specs=(P("dp", "mp"), P("dp", "mp")),
        check_vma=False,
    )
```

```python
import jax
import jax.numpy as jnp
from jax import lax
from jax.experimental import pallas as pl
from jax.experimental.pallas import tpu as pltpu
from jax.sharding import PartitionSpec as P

BAL = 208
BF = jnp.bfloat16
F32 = jnp.float32


def contract_last(left, right):
    return lax.dot_general(
        left, right, (((1,), (1,)), ((), ())), preferred_element_type=F32
    )


def contract_first(left, right):
    return lax.dot_general(
        left, right, (((0,), (0,)), ((), ())), preferred_element_type=F32
    )


def swiglu_back(x_rows, cot_rows, gate_full, up_full, live_mask):
    gate_val = jnp.dot(x_rows, gate_full, preferred_element_type=F32)
    up_val = jnp.dot(x_rows, up_full, preferred_element_type=F32)
    sig = jax.nn.sigmoid(gate_val)
    cot_val = cot_rows.astype(F32)
    d_gate = jnp.where(
        live_mask[:, None], cot_val * up_val * sig * (1.0 + gate_val * (1.0 - sig)), 0.0
    ).astype(BF)
    d_up = jnp.where(live_mask[:, None], cot_val * gate_val * sig, 0.0).astype(BF)
    return contract_last(d_gate, gate_full) + contract_last(d_up, up_full), d_gate


def live_rows_of(send_counts, recv_counts):
    return BAL + jnp.sum(send_counts[0]) - jnp.sum(recv_counts[0])


def general_plan(x_in, cotangent, w_gate, w_up, send_counts, recv_counts):
    dev_count = lax.axis_size("dp")
    gate_full = lax.all_gather(w_gate, "dp", axis=0, tiled=True)
    up_full = lax.all_gather(w_up, "dp", axis=0, tiled=True)
    live_mask = jnp.arange(x_in.shape[0]) < live_rows_of(send_counts, recv_counts)
    partial_value, d_gate = swiglu_back(x_in, cotangent, gate_full, up_full, live_mask)
    grad_x = lax.psum_scatter(
        partial_value.astype(BF), "mp", scatter_dimension=1, tiled=True
    )
    whole = contract_first(x_in, d_gate)
    pieces = lax.all_to_all(
        whole.reshape(dev_count, x_in.shape[1] // dev_count, whole.shape[1]),
        "dp",
        split_axis=0,
        concat_axis=0,
        tiled=True,
    )
    return grad_x, jnp.sum(pieces, axis=0)


PLANES = 4
PLACES = 4
TILE = 256


def tie(*values):
    return lax.optimization_barrier(values)


def chunk_kernel(scalars, mine_ref, other_ref, *refs, plan):
    groups = []
    for n, sizes in plan["counts"]:
        members = []
        for size in sizes:
            members.append(refs[:size])
            refs = refs[size:]
        groups.append((n, members))
    prev = None
    if not plan["first"]:
        prev, refs = refs[:2], refs[2:]
    gx_refs, refs = refs[:2], refs[2:]
    n_out = 1 if plan["last"] else PLANES
    gg_refs, (w_all, x_tile, cot_tile, acc) = refs[:n_out], refs[n_out:]
    step = pl.program_id(0)
    width, wide = w_all.shape
    ck = wide // 2
    blk = width // (PLANES * PLACES)
    half = width // 2
    rows = TILE // 2
    core = scalars[PLANES * PLACES]
    left = plan["left"]

    def place_rows(first_block, n, value):
        for i in range(n // blk):
            start = pl.multiple_of(scalars[first_block + i] * blk, blk)
            w_all[pl.ds(start, blk), :] = value(slice(i * blk, (i + 1) * blk))

    @pl.when(step == 0)
    def _():
        base = 0
        cols = slice(left, left + wide)
        for n, members in groups:
            for i, (value, *more) in enumerate(members):
                if more:
                    place_rows(i * PLACES + base, n, lambda r: value[r, cols] + more[0][r, cols])
                else:
                    place_rows(i * PLACES + base, n, lambda r: value[r, cols])
            base += n // blk

    lower = pl.ds(pl.multiple_of(core * rows, rows), rows)
    upper = pl.ds(pl.multiple_of((1 - core) * rows, rows), rows)
    x_tile[lower, :] = mine_ref[0, :, :width]
    x_tile[upper, :] = other_ref[0]
    for i in range(2):
        at_col = plan["cot"] + i * plan["quarter"] + plan["offset"]
        cot_tile[i * rows : (i + 1) * rows, :] = mine_ref[0, :, at_col : at_col + ck]

    x = x_tile[...]
    both = jnp.dot(x, w_all[...], preferred_element_type=F32)
    gate, up = both[:, :ck], both[:, ck:]
    cot = cot_tile[...].astype(F32)
    sig = jax.nn.sigmoid(gate)
    d_gate = (cot * up * sig * (1.0 + gate * (1.0 - sig))).astype(BF)
    d_up = (cot * gate * sig).astype(BF)
    gg = contract_first(x, d_gate)

    @pl.when(step == 0)
    def _():
        acc[...] = gg

    @pl.when(step > 0)
    def _():
        acc[...] += gg

    gx = contract_last(jnp.concatenate([d_gate, d_up], axis=1), w_all[...])
    low, high = gx[:, :half], gx[:, half:]
    for keep in range(2):

        @pl.when(core == keep)
        def _():
            for ref, value, i in ((gx_refs[0], (low, high)[keep], 0), (gx_refs[1], (high, low)[keep], 1)):
                ref[...] = (value if prev is None else value + prev[i][...].astype(F32)).astype(BF)

    @pl.when(step == pl.num_programs(0) - 1)
    def _():
        for j in range(PLANES * PLACES):
            if plan["last"]:
                gg_refs[0][j] = acc[j * blk : (j + 1) * blk, :].astype(BF)
            else:
                start = pl.multiple_of(scalars[j] * blk, blk)
                row = (j % PLACES) * blk
                gg_refs[j // PLACES][row : row + blk, :] = acc[pl.ds(start, blk), :].astype(BF)


def chunk_call(scalars, mine, other, groups, prev, ck, **plan):
    width = other.shape[2]
    rows = PLACES * TILE
    half = width // 2
    plan["counts"] = [(g[0][0].shape[0], [len(m) for m in g]) for g in groups]
    flat = [v for g in groups for m in g for v in m]
    plan["first"] = prev is None
    blk = width // (PLANES * PLACES)
    deep = width // PLANES
    gx_spec = pl.BlockSpec((TILE, half), lambda i, o: (i, 0))
    w_specs = [
        pl.BlockSpec(v.shape, lambda i, o: (0, 0), pipeline_mode=pl.Buffered(1))
        for v in flat
    ]
    if plan["last"]:
        gg_specs = [pl.BlockSpec((PLANES * PLACES, blk, ck), lambda i, o: (0, 0, 0))]
        gg_shapes = [jax.ShapeDtypeStruct((PLANES * PLACES, blk, ck), BF)]
    else:
        gg_specs = [pl.BlockSpec((deep, ck), lambda i, o: (0, 0))] * PLANES
        gg_shapes = [jax.ShapeDtypeStruct((deep, ck), BF)] * PLANES
    outs = pl.pallas_call(
        lambda *a: chunk_kernel(*a, plan=plan),
        grid_spec=pltpu.PrefetchScalarGridSpec(
            num_scalar_prefetch=1,
            grid=(PLACES,),
            in_specs=[
                pl.BlockSpec((1,) + mine.shape[1:], lambda i, o: (i, 0, 0)),
                pl.BlockSpec((1,) + other.shape[1:], lambda i, o: (i, 0, 0)),
            ]
            + w_specs
            + ([] if prev is None else [gx_spec] * 2),
            out_specs=[gx_spec] * 2 + gg_specs,
            scratch_shapes=[
                pltpu.VMEM((width, 2 * ck), BF),
                pltpu.VMEM((TILE, width), BF),
                pltpu.VMEM((TILE, ck), BF),
                pltpu.VMEM((width, ck), F32),
            ],
        ),
        out_shape=[jax.ShapeDtypeStruct((rows, half), BF)] * 2 + gg_shapes,
        compiler_params=pltpu.CompilerParams(vmem_limit_bytes=56 * 1024 * 1024),
        cost_estimate=pl.CostEstimate(
            flops=10 * rows * width * ck, bytes_accessed=2**24, transcendentals=rows * ck
        ),
        name="swiglu_chunk",
    )(scalars, mine, other, *flat, *([] if prev is None else prev))
    return outs[:2], outs[2:]


def join_kernel(scalars, *refs, widths, quarter):
    out = refs[-1]
    firsts, last = refs[:PLACES], refs[PLACES]
    split = widths[0]
    for s in range(PLACES):
        start = scalars[PLANES * PLACES + 1 + s] * quarter
        spot = pl.ds(pl.multiple_of(start, 128), split)
        out[:, spot] = firsts[s][...].astype(F32)
    for q in range(PLACES):
        total = last[q].astype(F32)
        for z in range(1, PLANES):
            total = total + last[z * PLACES + q].astype(F32)
        out[:, q * quarter + split : (q + 1) * quarter] = total


def join_call(scalars, firsts, last, widths, quarter):
    depth = last.shape[1]
    vmem = pl.BlockSpec(memory_space=pltpu.VMEM)
    return pl.pallas_call(
        lambda *a: join_kernel(*a, widths=widths, quarter=quarter),
        in_specs=[pl.BlockSpec(memory_space=pltpu.SMEM)] + [vmem] * (PLACES + 1),
        out_specs=vmem,
        out_shape=jax.ShapeDtypeStruct((depth, PLACES * quarter), F32),
        compiler_params=pltpu.CompilerParams(vmem_limit_bytes=16 * 1024 * 1024),
        name="join_chunks",
    )(scalars, *firsts, last)


def at(z, q):
    return z * PLACES + q


def pairs_in_plane(s):
    return [(at(z, q), at(z, q ^ s)) for z in range(PLANES) for q in range(PLACES)]


def pairs_across(r):
    return [(at(z, q), at(z ^ r, q)) for z in range(PLANES) for q in range(PLACES)]


def pairs_of_planes(moves):
    return [(at(a, q), at(b, q)) for a, b in moves for q in range(PLACES)]


OUTER = pairs_of_planes([(0, 1), (1, 0), (2, 3), (3, 2)])
INNER = pairs_of_planes([(1, 2), (2, 1)])
TO_ENDS = pairs_of_planes([(1, 0), (2, 3)])
FROM_ENDS = pairs_of_planes([(0, 1), (3, 2)])
COLUMN_GROUPS = [[at(z, q) for z in range(PLANES)] for q in range(PLACES)]


def send(value, pairs):
    return lax.ppermute(value, "dp", pairs)


def from_plane(pieces):
    return [send(p, pairs_in_plane(s)) if s else p for s, p in enumerate(pieces)]


def gather_planes(own):
    a1 = send(own, OUTER)
    b1 = send(own, INNER)
    a2 = send(a1, INNER)
    b2 = send(b1, TO_ENDS)
    a3 = send(a2, TO_ENDS)
    return own, a1, b1, b2, a2, a3


def plane_order(z):
    low = z < 2
    return [z, z ^ 1, jnp.where(low, 2, 1), jnp.where(low, 3, 0)]


def add(*terms):
    total = terms[0].astype(F32)
    for term in terms[1:]:
        total = total + term.astype(F32)
    return total.astype(BF)


def sum_planes(parts):
    own, p1, p2, p3 = parts
    r1 = send(p3, FROM_ENDS)
    r2b = send(p2, FROM_ENDS)
    r2a = send(add(p3, r1), INNER)
    r3b = send(add(p2, r2b), INNER)
    r3a = send(add(p1, r2a), OUTER)
    return add(own, r3a, r3b)


def planes_plan(x_in, cotangent, w_gate, w_up, send_counts, recv_counts):
    rows, width = x_in.shape
    depth, hidden = w_gate.shape
    quarter = hidden // PLACES
    half = width // 2
    core = lax.axis_index("mp")
    index = lax.axis_index("dp")
    z, place = index // PLACES, index % PLACES
    chunks = [640, 256]
    swap = [(0, 1), (1, 0)]
    offsets = [sum(chunks[:i]) for i in range(len(chunks))]

    def columns(array, q, offset, count):
        return lax.dynamic_slice_in_dim(array, q * quarter + offset, count, 1)

    def piece_of_weights(q, which):
        return jnp.concatenate(
            [columns(w, q, offsets[k], chunks[k]) for k in which for w in (w_gate, w_up)], axis=1
        )

    def scalars_for(order):
        return jnp.stack(
            [order[r] * PLACES + (place ^ s) for r in range(PLANES) for s in range(PLACES)]
            + [core]
            + [place ^ s for s in range(PLACES)]
        ).astype(jnp.int32)

    relayed = scalars_for(plane_order(z))
    direct = scalars_for([z ^ r for r in range(PLANES)])

    first = [piece_of_weights(place ^ s, (0,)) for s in range(PLACES)]
    own = first[0]
    a1o = send(own, OUTER)
    b1o = send(own, INNER)
    rest = from_plane(first)[1:]
    a2o = send(a1o, INNER)
    b2o = send(b1o, TO_ENDS)
    a2o, b2o, x_in, cotangent, w_gate, w_up, *rest = tie(
        a2o, b2o, x_in, cotangent, w_gate, w_up, *rest
    )

    rest = jnp.concatenate(rest, axis=0)
    a1r = send(rest, OUTER)
    b1r = send(rest, INNER)
    a3o = send(a2o, TO_ENDS)
    live = jnp.arange(rows) < live_rows_of(send_counts, recv_counts)
    cotangent = jnp.where(live[:, None], cotangent, jnp.zeros((), BF))
    x_half = lax.dynamic_slice_in_dim(x_in, core * (rows // 2), rows // 2, 0)
    parcels = []
    for s in range(PLACES):
        cot = columns(cotangent, place ^ s, 0, quarter)
        parcels.append(
            jnp.concatenate(
                [x_half, cot[: rows // 2], cot[rows // 2 :], piece_of_weights(place ^ s, (1,))],
                axis=1,
            )
        )
    parcels = from_plane(parcels)
    a1r, b1r, a3o = tie(a1r, b1r, a3o)

    a2r = send(a1r, INNER)
    b2r = send(b1r, TO_ENDS)
    a2r, b2r, *parcels = tie(a2r, b2r, *parcels)
    mine = jnp.stack(parcels)
    other = lax.ppermute(mine[:, :, :width], "mp", swap)
    cot_at = width
    last_at = width + 2 * quarter

    second = mine[:, :, last_at:].reshape(PLACES * depth, 2 * chunks[1])
    a3r = send(a2r, TO_ENDS)
    a3r, other, second = tie(a3r, other, second)

    common = dict(cot=width, quarter=quarter)
    near = send(second, pairs_across(1))
    far = send(second, pairs_across(2))
    gx, parts = chunk_call(
        relayed, mine, other,
        [
            ((own,), (a1o,), (b1o, b2o), (a2o, a3o)),
            ((rest,), (a1r,), (b1r, b2r), (a2r, a3r)),
        ],
        None, chunks[0], left=0, offset=0, last=False, **common,
    )
    near, far, *values = tie(near, far, *gx, *parts)
    gx, (p0, p1, p2, p3) = values[:2], values[2:]
    r1 = send(p3, FROM_ENDS)
    middle = send(second, INNER)
    ends = send(far, TO_ENDS)
    r1, middle, ends, p2, p3 = tie(r1, middle, ends, p2, p3)
    r2b = send(p2, FROM_ENDS)
    r2a = send(add(p3, r1), INNER)
    (keep, give), (lasts,) = chunk_call(
        direct, mine, other, [((second,), (near,), (far,), (middle, ends))], gx, chunks[1],
        left=0, offset=offsets[1], last=True, **common,
    )
    r2a, r2b, keep, give, lasts = tie(r2a, r2b, keep, give, lasts)
    lasts = lax.all_to_all(lasts, "dp", split_axis=0, concat_axis=0, tiled=True)
    theirs = lax.ppermute(give, "mp", swap)
    r3b = send(add(p2, r2b), INNER)
    r3a = send(add(p1, r2a), OUTER)
    rows_x = from_plane(
        [
            add(keep[s * rows : (s + 1) * rows], theirs[s * rows : (s + 1) * rows])
            for s in range(PLACES)
        ]
    )
    r3a, r3b, *rows_x = tie(r3a, r3b, *rows_x)
    sums = add(p0, r3a, r3b)
    firsts = from_plane([sums[s * depth : (s + 1) * depth] for s in range(PLACES)])
    grad_gate = join_call(relayed, firsts, lasts, [chunks[0]], quarter)
    return add(*rows_x), grad_gate


def solution(mesh):
    sizes = dict(mesh.shape)
    by_planes = sizes["dp"] == PLANES * PLACES and sizes["mp"] == 2
    return jax.shard_map(
        planes_plan if by_planes else general_plan,
        mesh=mesh,
        in_specs=(
            P("dp", None),
            P("dp", "mp"),
            P("dp", "mp"),
            P("dp", "mp"),
            P("dp", None),
            P("dp", None),
        ),
        out_specs=(P("dp", "mp"), P("dp", "mp")),
        check_vma=False,
    )
```

```python
import jax
import jax.numpy as jnp
from jax import lax
from jax.experimental import pallas as pl
from jax.experimental.pallas import tpu as pltpu
from jax.sharding import PartitionSpec as P

BAL = 208
BF = jnp.bfloat16
F32 = jnp.float32


def contract_last(left, right):
    return lax.dot_general(
        left, right, (((1,), (1,)), ((), ())), preferred_element_type=F32
    )


def contract_first(left, right):
    return lax.dot_general(
        left, right, (((0,), (0,)), ((), ())), preferred_element_type=F32
    )


def swiglu_back(x_rows, cot_rows, gate_full, up_full, live_mask):
    gate_val = jnp.dot(x_rows, gate_full, preferred_element_type=F32)
    up_val = jnp.dot(x_rows, up_full, preferred_element_type=F32)
    sig = jax.nn.sigmoid(gate_val)
    cot_val = cot_rows.astype(F32)
    d_gate = jnp.where(
        live_mask[:, None], cot_val * up_val * sig * (1.0 + gate_val * (1.0 - sig)), 0.0
    ).astype(BF)
    d_up = jnp.where(live_mask[:, None], cot_val * gate_val * sig, 0.0).astype(BF)
    return contract_last(d_gate, gate_full) + contract_last(d_up, up_full), d_gate


def live_rows_of(send_counts, recv_counts):
    return BAL + jnp.sum(send_counts[0]) - jnp.sum(recv_counts[0])


def general_plan(x_in, cotangent, w_gate, w_up, send_counts, recv_counts):
    dev_count = lax.axis_size("dp")
    gate_full = lax.all_gather(w_gate, "dp", axis=0, tiled=True)
    up_full = lax.all_gather(w_up, "dp", axis=0, tiled=True)
    live_mask = jnp.arange(x_in.shape[0]) < live_rows_of(send_counts, recv_counts)
    partial_value, d_gate = swiglu_back(x_in, cotangent, gate_full, up_full, live_mask)
    grad_x = lax.psum_scatter(
        partial_value.astype(BF), "mp", scatter_dimension=1, tiled=True
    )
    whole = contract_first(x_in, d_gate)
    pieces = lax.all_to_all(
        whole.reshape(dev_count, x_in.shape[1] // dev_count, whole.shape[1]),
        "dp",
        split_axis=0,
        concat_axis=0,
        tiled=True,
    )
    return grad_x, jnp.sum(pieces, axis=0)


CREW = (0, 1, 2, 3)
NEAR, FAR = 4, 8
CHAIN = (0, NEAR, FAR, NEAR | FAR)
DEVS = 16
TILE = 256


def tie(*values):
    return lax.optimization_barrier(values)


def send(value, mask):
    return lax.ppermute(value, "dp", [(i, i ^ mask) for i in range(DEVS)])


def along(value, moves):
    crew = len(CREW)
    return lax.ppermute(
        value, "dp", [(crew * a + q, crew * b + q) for a, b in moves for q in range(crew)]
    )


OUTER = [(0, 1), (1, 0), (2, 3), (3, 2)]
INNER = [(1, 2), (2, 1)]
TO_ENDS = [(1, 0), (2, 3)]
FROM_ENDS = [(0, 1), (3, 2)]


def crew_swap(pieces):
    return [send(p, m) if m else p for p, m in zip(pieces, CREW)]


def add(*terms):
    total = terms[0].astype(F32)
    for term in terms[1:]:
        total = total + term.astype(F32)
    return total.astype(BF)


def chunk_kernel(scalars, mine_ref, other_ref, *refs, plan):
    groups = []
    for n, members in plan["counts"]:
        groups.append((n, refs[:members]))
        refs = refs[members:]
    prev = None
    if not plan["first"]:
        prev, refs = refs[:2], refs[2:]
    gx_refs, refs = refs[:2], refs[2:]
    n_out = 1 if plan["last"] else len(CHAIN)
    gg_refs, (w_all, x_tile, cot_tile, acc, sems) = refs[:n_out], refs[n_out:]
    step = pl.program_id(0)
    width, wide = w_all.shape
    ck = wide // 2
    blk = width // DEVS
    crew = len(CREW)
    half = width // 2
    rows = TILE // 2
    core = scalars[DEVS]

    def block_rows(j):
        return pl.ds(pl.multiple_of(scalars[j] * blk, blk), blk)

    inner = scalars[DEVS + 1]

    def weight_copies(act):
        base = 0
        for n, members in groups:
            for c, member in enumerate(members):
                for i in range(n // blk):
                    j = min(c, len(CHAIN) - 1) * crew + base + i
                    copy = pltpu.make_async_copy(
                        member.at[pl.ds(i * blk, blk), :], w_all.at[block_rows(j), :], sems.at[j]
                    )
                    if len(members) > len(CHAIN) and c >= len(CHAIN) - 1:
                        pl.when(inner == (1 if c == len(CHAIN) - 1 else 0))(
                            lambda copy=copy: act(copy)
                        )
                    else:
                        act(copy)
            base += n // blk

    @pl.when(step == 0)
    def _():
        weight_copies(lambda copy: copy.start())

    lower = pl.ds(pl.multiple_of(core * rows, rows), rows)
    upper = pl.ds(pl.multiple_of((1 - core) * rows, rows), rows)
    x_tile[lower, :] = mine_ref[0, :, :width]
    x_tile[upper, :] = other_ref[0]
    for i in range(2):
        at_col = plan["cot"] + i * plan["quarter"] + plan["offset"]
        cot_tile[i * rows : (i + 1) * rows, :] = mine_ref[0, :, at_col : at_col + ck]

    @pl.when(step == 0)
    def _():
        weight_copies(lambda copy: copy.wait())

    x = x_tile[...]
    both = jnp.dot(x, w_all[...], preferred_element_type=F32)
    gate, up = both[:, :ck], both[:, ck:]
    cot = cot_tile[...].astype(F32)
    sig = jax.nn.sigmoid(gate)
    d_gate = (cot * up * sig * (1.0 + gate * (1.0 - sig))).astype(BF)
    d_up = (cot * gate * sig).astype(BF)
    gg = contract_first(x, d_gate)

    @pl.when(step == 0)
    def _():
        acc[...] = gg

    @pl.when(step > 0)
    def _():
        acc[...] += gg

    gx = contract_last(jnp.concatenate([d_gate, d_up], axis=1), w_all[...])
    low, high = gx[:, :half], gx[:, half:]
    for keep in range(2):

        @pl.when(core == keep)
        def _():
            for ref, value, i in ((gx_refs[0], (low, high)[keep], 0), (gx_refs[1], (high, low)[keep], 1)):
                ref[...] = (value if prev is None else value + prev[i][...].astype(F32)).astype(BF)

    @pl.when(step == pl.num_programs(0) - 1)
    def _():
        for j in range(DEVS):
            if plan["last"]:
                gg_refs[0][j] = acc[j * blk : (j + 1) * blk, :].astype(BF)
            else:
                row = (j % crew) * blk
                at_row = pl.multiple_of(scalars[2 * DEVS + j] * blk, blk)
                gg_refs[j // crew][row : row + blk, :] = acc[pl.ds(at_row, blk), :].astype(BF)


def chunk_call(scalars, mine, other, groups, prev, ck, **plan):
    width = other.shape[2]
    rows = len(CREW) * TILE
    half = width // 2
    plan["counts"] = [(g[0].shape[0], len(g)) for g in groups]
    plan["first"] = prev is None
    flat = [v for g in groups for v in g]
    blk = width // DEVS
    deep = blk * len(CREW)
    gx_spec = pl.BlockSpec((TILE, half), lambda i, o: (i, 0))
    if plan["last"]:
        gg_specs = [pl.BlockSpec((DEVS, blk, ck), lambda i, o: (0, 0, 0))]
        gg_shapes = [jax.ShapeDtypeStruct((DEVS, blk, ck), BF)]
    else:
        gg_specs = [pl.BlockSpec((deep, ck), lambda i, o: (0, 0))] * len(CHAIN)
        gg_shapes = [jax.ShapeDtypeStruct((deep, ck), BF)] * len(CHAIN)
    outs = pl.pallas_call(
        lambda *a: chunk_kernel(*a, plan=plan),
        grid_spec=pltpu.PrefetchScalarGridSpec(
            num_scalar_prefetch=1,
            grid=(len(CREW),),
            in_specs=[
                pl.BlockSpec((1,) + mine.shape[1:], lambda i, o: (i, 0, 0)),
                pl.BlockSpec((1,) + other.shape[1:], lambda i, o: (i, 0, 0)),
            ]
            + [pl.BlockSpec(memory_space=pl.ANY)] * len(flat)
            + ([] if prev is None else [gx_spec] * 2),
            out_specs=[gx_spec] * 2 + gg_specs,
            scratch_shapes=[
                pltpu.VMEM((width, 2 * ck), BF),
                pltpu.VMEM((TILE, width), BF),
                pltpu.VMEM((TILE, ck), BF),
                pltpu.VMEM((width, ck), F32),
                pltpu.SemaphoreType.DMA((DEVS,)),
            ],
        ),
        out_shape=[jax.ShapeDtypeStruct((rows, half), BF)] * 2 + gg_shapes,
        compiler_params=pltpu.CompilerParams(vmem_limit_bytes=48 * 1024 * 1024),
        cost_estimate=pl.CostEstimate(
            flops=10 * rows * width * ck, bytes_accessed=2**24, transcendentals=rows * ck
        ),
        name="swiglu_chunk",
    )(scalars, mine, other, *flat, *([] if prev is None else prev))
    return outs[:2], outs[2:]


def join_kernel(scalars, *refs, split, quarter):
    out = refs[-1]
    firsts, last = refs[: len(CREW)], refs[len(CREW)]
    for s in range(len(CREW)):
        start = scalars[DEVS + 2 + s] * quarter
        spot = pl.ds(pl.multiple_of(start, 128), split)
        out[:, spot] = firsts[s][...].astype(F32)
    for q in range(len(CREW)):
        total = None
        for m in CHAIN:
            term = last[q ^ m].astype(F32)
            total = term if total is None else total + term
        out[:, q * quarter + split : (q + 1) * quarter] = total


def join_call(scalars, firsts, last, split, quarter):
    depth = last.shape[1]
    vmem = pl.BlockSpec(memory_space=pltpu.VMEM)
    return pl.pallas_call(
        lambda *a: join_kernel(*a, split=split, quarter=quarter),
        in_specs=[pl.BlockSpec(memory_space=pltpu.SMEM)] + [vmem] * (len(CREW) + 1),
        out_specs=vmem,
        out_shape=jax.ShapeDtypeStruct((depth, len(CREW) * quarter), F32),
        compiler_params=pltpu.CompilerParams(vmem_limit_bytes=16 * 1024 * 1024),
        name="join_chunks",
    )(scalars, *firsts, last)


def split_plan(x_in, cotangent, w_gate, w_up, send_counts, recv_counts):
    rows, width = x_in.shape
    depth, hidden = w_gate.shape
    crew = len(CREW)
    quarter = hidden // crew
    core = lax.axis_index("mp")
    index = lax.axis_index("dp")
    z, place = index // crew, index % crew
    places = [place ^ m for m in CREW]
    chunks = [640, 256]
    offsets = [0, chunks[0]]
    swap = [(0, 1), (1, 0)]

    def columns(array, q, offset, count):
        return lax.dynamic_slice_in_dim(array, q * quarter + offset, count, 1)

    def piece_of_weights(q, k):
        return jnp.concatenate(
            [columns(w, q, offsets[k], chunks[k]) for w in (w_gate, w_up)], axis=1
        )

    order = [z, z ^ 1, jnp.where(z < 2, 2, 1), jnp.where(z < 2, 3, 0)]
    inner = ((z == 1) | (z == 2)).astype(jnp.int32)
    scalars = [index ^ c ^ m for c in CHAIN for m in CREW] + [core, inner] + places
    scalars += [0] * (2 * DEVS - len(scalars)) + [p * crew + q for p in order for q in places]
    scalars = jnp.stack([jnp.asarray(v, jnp.int32) for v in scalars])

    first = [piece_of_weights(q, 0) for q in places]
    own = first[0]
    own_far = send(own, FAR)
    own_near = send(own, NEAR)
    rest = crew_swap(first)[1:]
    own_far, own_near, x_in, cotangent, w_gate, w_up, *rest = tie(
        own_far, own_near, x_in, cotangent, w_gate, w_up, *rest
    )

    rest = jnp.concatenate(rest, axis=0)
    own_both = send(own_far, NEAR)
    rest_far = send(rest, FAR)
    rest_near = send(rest, NEAR)
    live = jnp.arange(rows) < live_rows_of(send_counts, recv_counts)
    cotangent = jnp.where(live[:, None], cotangent, jnp.zeros((), BF))
    x_half = lax.dynamic_slice_in_dim(x_in, core * (rows // 2), rows // 2, 0)
    parcels = []
    for q in places:
        cot = columns(cotangent, q, 0, quarter)
        parcels.append(
            jnp.concatenate(
                [x_half, cot[: rows // 2], cot[rows // 2 :], piece_of_weights(q, 1)], axis=1
            )
        )
    parcels = crew_swap(parcels)
    rest_far, rest_near, own_both, *parcels = tie(rest_far, rest_near, own_both, *parcels)

    rest_both = send(rest_far, NEAR)
    mine = jnp.stack(parcels)
    other = lax.ppermute(mine[:, :, :width], "mp", swap)
    second = mine[:, :, width + 2 * quarter :].reshape(crew * depth, 2 * chunks[1])
    rest_both, other, second = tie(rest_both, other, second)

    common = dict(cot=width, quarter=quarter)
    second_near = send(second, NEAR)
    second_far = send(second, FAR)
    gx, parts = chunk_call(
        scalars, mine, other,
        [(own, own_near, own_far, own_both), (rest, rest_near, rest_far, rest_both)],
        None, chunks[0], offset=0, last=False, **common,
    )
    second_near, second_far, *values = tie(second_near, second_far, *gx, *parts)
    gx, (p0, p1, p2, p3) = values[:2], values[2:]

    middle = along(second, INNER)
    ends = along(second_far, TO_ENDS)
    r1 = along(p3, FROM_ENDS)
    r1, middle, ends, p2, p3 = tie(r1, middle, ends, p2, p3)
    r2b = along(p2, FROM_ENDS)
    r2a = along(add(p3, r1), INNER)
    (keep, give), (lasts,) = chunk_call(
        scalars, mine, other, [(second, second_near, second_far, middle, ends)], gx, chunks[1],
        offset=offsets[1], last=True, **common,
    )
    r2a, r2b, keep, give, lasts = tie(r2a, r2b, keep, give, lasts)

    lasts = lax.all_to_all(lasts, "dp", split_axis=0, concat_axis=0, tiled=True)
    theirs = lax.ppermute(give, "mp", swap)
    r3b = along(add(p2, r2b), INNER)
    r3a = along(add(p1, r2a), OUTER)
    rows_x = crew_swap(
        [
            add(keep[s * rows : (s + 1) * rows], theirs[s * rows : (s + 1) * rows])
            for s in range(crew)
        ]
    )
    r3a, r3b, *rows_x = tie(r3a, r3b, *rows_x)

    sums = add(p0, r3a, r3b)
    firsts = crew_swap([sums[s * depth : (s + 1) * depth] for s in range(crew)])
    grad_gate = join_call(scalars, firsts, lasts, chunks[0], quarter)
    return add(*rows_x), grad_gate


def solution(mesh):
    sizes = dict(mesh.shape)
    splits = sizes["dp"] == DEVS and sizes["mp"] == 2
    return jax.shard_map(
        split_plan if splits else general_plan,
        mesh=mesh,
        in_specs=(
            P("dp", None),
            P("dp", "mp"),
            P("dp", "mp"),
            P("dp", "mp"),
            P("dp", None),
            P("dp", None),
        ),
        out_specs=(P("dp", "mp"), P("dp", "mp")),
        check_vma=False,
    )
```

```python
import jax
import jax.numpy as jnp
from jax import lax
from jax.experimental import pallas as pl
from jax.experimental.pallas import tpu as pltpu
from jax.sharding import PartitionSpec as P

BAL = 208
BF = jnp.bfloat16
F32 = jnp.float32


def contract_last(left, right):
    return lax.dot_general(
        left, right, (((1,), (1,)), ((), ())), preferred_element_type=F32
    )


def contract_first(left, right):
    return lax.dot_general(
        left, right, (((0,), (0,)), ((), ())), preferred_element_type=F32
    )


def swiglu_back(x_rows, cot_rows, gate_full, up_full, live_mask):
    gate_val = jnp.dot(x_rows, gate_full, preferred_element_type=F32)
    up_val = jnp.dot(x_rows, up_full, preferred_element_type=F32)
    sig = jax.nn.sigmoid(gate_val)
    cot_val = cot_rows.astype(F32)
    d_gate = jnp.where(
        live_mask[:, None], cot_val * up_val * sig * (1.0 + gate_val * (1.0 - sig)), 0.0
    ).astype(BF)
    d_up = jnp.where(live_mask[:, None], cot_val * gate_val * sig, 0.0).astype(BF)
    return contract_last(d_gate, gate_full) + contract_last(d_up, up_full), d_gate


def live_rows_of(send_counts, recv_counts):
    return BAL + jnp.sum(send_counts[0]) - jnp.sum(recv_counts[0])


def general_plan(x_in, cotangent, w_gate, w_up, send_counts, recv_counts):
    dev_count = lax.axis_size("dp")
    gate_full = lax.all_gather(w_gate, "dp", axis=0, tiled=True)
    up_full = lax.all_gather(w_up, "dp", axis=0, tiled=True)
    live_mask = jnp.arange(x_in.shape[0]) < live_rows_of(send_counts, recv_counts)
    partial_value, d_gate = swiglu_back(x_in, cotangent, gate_full, up_full, live_mask)
    grad_x = lax.psum_scatter(
        partial_value.astype(BF), "mp", scatter_dimension=1, tiled=True
    )
    whole = contract_first(x_in, d_gate)
    pieces = lax.all_to_all(
        whole.reshape(dev_count, x_in.shape[1] // dev_count, whole.shape[1]),
        "dp",
        split_axis=0,
        concat_axis=0,
        tiled=True,
    )
    return grad_x, jnp.sum(pieces, axis=0)


CREW = (0, 1, 2, 3)
NEAR, FAR = 4, 8
CHAIN = (0, NEAR, FAR, NEAR | FAR)
DEVS = 16
TILE = 256


def tie(*values):
    return lax.optimization_barrier(values)


def send(value, mask):
    return lax.ppermute(value, "dp", [(i, i ^ mask) for i in range(DEVS)])


def along(value, moves):
    crew = len(CREW)
    return lax.ppermute(
        value, "dp", [(crew * a + q, crew * b + q) for a, b in moves for q in range(crew)]
    )


OUTER = [(0, 1), (1, 0), (2, 3), (3, 2)]
INNER = [(1, 2), (2, 1)]
TO_ENDS = [(1, 0), (2, 3)]
FROM_ENDS = [(0, 1), (3, 2)]


def crew_swap(pieces):
    return [send(p, m) if m else p for p, m in zip(pieces, CREW)]


def add(*terms):
    total = terms[0].astype(F32)
    for term in terms[1:]:
        total = total + term.astype(F32)
    return total.astype(BF)


def place_weights(scalars, groups, w_all, sems, act):
    blk = w_all.shape[0] // DEVS
    crew = len(CREW)
    inner = scalars[DEVS + 1]
    base = 0
    for n, members in groups:
        for c, member in enumerate(members):
            for i in range(n // blk):
                j = min(c, len(CHAIN) - 1) * crew + base + i
                start = pl.multiple_of(scalars[j] * blk, blk)
                copy = pltpu.make_async_copy(
                    member.at[pl.ds(i * blk, blk), :], w_all.at[pl.ds(start, blk), :], sems.at[j]
                )
                if len(members) > len(CHAIN) and c >= len(CHAIN) - 1:
                    pl.when(inner == (1 if c == len(CHAIN) - 1 else 0))(
                        lambda copy=copy: act(copy)
                    )
                else:
                    act(copy)
        base += n // blk


def grouped(refs, counts):
    groups = []
    for n, members in counts:
        groups.append((n, refs[:members]))
        refs = refs[members:]
    return groups, refs


def place_rows(core, tile, mine_ref, other_ref, cols=slice(None)):
    rows = TILE // 2
    lower = pl.ds(pl.multiple_of(core * rows, rows), rows)
    upper = pl.ds(pl.multiple_of((1 - core) * rows, rows), rows)
    tile[lower, :] = mine_ref[0, :, cols]
    tile[upper, :] = other_ref[0, :, cols]


def store_rows_grad(core, gx, gx_refs, prev):
    half = gx.shape[1] // 2
    low, high = gx[:, :half], gx[:, half:]
    for keep in range(2):

        @pl.when(core == keep)
        def _():
            for i, value in enumerate(((low, high)[keep], (high, low)[keep])):
                if prev is not None:
                    value = value + prev[i][...].astype(F32)
                gx_refs[i][...] = value.astype(BF)


def front(x, w_all, cot_lower, cot_upper):
    ck = w_all.shape[1] // 2
    both = jnp.dot(x, w_all[...], preferred_element_type=F32)
    gate, up = both[:, :ck], both[:, ck:]
    cot = jnp.concatenate([cot_lower, cot_upper], axis=0).astype(F32)
    sig = jax.nn.sigmoid(gate)
    d_gate = (cot * up * sig * (1.0 + gate * (1.0 - sig))).astype(BF)
    d_up = (cot * gate * sig).astype(BF)
    return d_gate, d_up


def first_kernel(scalars, mine_ref, other_ref, low_ref, high_ref, *refs, counts):
    groups, refs = grouped(refs, counts)
    d_ref, refs = refs[0], refs[1:]
    gg_refs, (w_all, x_all, d_all, acc, sems) = refs[: len(CHAIN)], refs[len(CHAIN) :]
    step = pl.program_id(0)
    width = w_all.shape[0]
    blk = width // DEVS
    crew = len(CREW)

    @pl.when(step == 0)
    def _():
        place_weights(scalars, groups, w_all, sems, lambda copy: copy.start())

    here = pl.ds(pl.multiple_of(step * TILE, TILE), TILE)
    place_rows(scalars[DEVS], x_all.at[here], mine_ref, other_ref)

    @pl.when(step == 0)
    def _():
        place_weights(scalars, groups, w_all, sems, lambda copy: copy.wait())

    d_gate, d_up = front(x_all[here, :], w_all, low_ref[0], high_ref[0])
    d_all[here, :] = d_gate
    d_ref[...] = jnp.concatenate([d_gate, d_up], axis=1)

    @pl.when(step == pl.num_programs(0) - 1)
    def _():
        d = d_all[...]
        deep = crew * blk
        for r in range(len(CHAIN)):
            cols = slice(r * deep, (r + 1) * deep)
            acc[cols, :] = contract_first(x_all[:, cols], d).astype(BF)
        for j in range(DEVS):
            row = (j % crew) * blk
            at_row = pl.multiple_of(scalars[2 * DEVS + j] * blk, blk)
            gg_refs[j // crew][row : row + blk, :] = acc[pl.ds(at_row, blk), :]


def rows_grad_kernel(scalars, d_ref, *refs, counts):
    groups, refs = grouped(refs, counts)
    gx_refs, (w_all, sems) = refs[:2], refs[2:]

    @pl.when(pl.program_id(0) == 0)
    def _():
        place_weights(scalars, groups, w_all, sems, lambda copy: copy.start())
        place_weights(scalars, groups, w_all, sems, lambda copy: copy.wait())

    store_rows_grad(scalars[DEVS], contract_last(d_ref[...], w_all[...]), gx_refs, None)


def second_kernel(scalars, mine_ref, other_ref, cot_ref, *refs, counts):
    groups, refs = grouped(refs, counts)
    prev, gx_refs, (d_ref, w_all, x_tile, sems) = refs[:2], refs[2:4], refs[4:]
    step = pl.program_id(0)
    ck = d_ref.shape[1]

    @pl.when(step == 0)
    def _():
        place_weights(scalars, groups, w_all, sems, lambda copy: copy.start())

    place_rows(scalars[DEVS], x_tile, mine_ref, other_ref)

    @pl.when(step == 0)
    def _():
        place_weights(scalars, groups, w_all, sems, lambda copy: copy.wait())

    d_gate, d_up = front(x_tile[...], w_all, cot_ref[0, :, :ck], cot_ref[0, :, ck:])
    d_ref[...] = d_gate
    gx = contract_last(jnp.concatenate([d_gate, d_up], axis=1), w_all[...])
    store_rows_grad(scalars[DEVS], gx, gx_refs, prev)


def gate_grad_kernel(scalars, mine_ref, other_ref, d_ref, *refs):
    out_refs, (x_all, acc) = refs[: len(CHAIN)], refs[len(CHAIN) :]
    step = pl.program_id(0)
    core = scalars[DEVS]
    crew = len(CREW)
    for s in range(crew):
        tile = x_all.at[s * TILE : (s + 1) * TILE]
        place_rows(core, tile, mine_ref.at[s : s + 1], other_ref.at[s : s + 1])
    deep = x_all.shape[1]
    here = pl.ds(pl.multiple_of(step * deep, deep), deep)
    acc[here, :] = contract_first(x_all[...], d_ref[...]).astype(BF)

    @pl.when(step == pl.num_programs(0) - 1)
    def _():
        blk = deep // crew
        for j in range(DEVS):
            row = (j % crew) * blk
            at_row = pl.multiple_of(scalars[j] * blk, blk)
            out_refs[j // crew][row : row + blk, :] = acc[pl.ds(at_row, blk), :]


def kernel_call(body, name, scalars, operands, in_specs, out_specs, out_shape, scratch, flops, limit):
    return pl.pallas_call(
        body,
        grid_spec=pltpu.PrefetchScalarGridSpec(
            num_scalar_prefetch=1,
            grid=(len(CREW),),
            in_specs=in_specs,
            out_specs=out_specs,
            scratch_shapes=scratch,
        ),
        out_shape=out_shape,
        compiler_params=pltpu.CompilerParams(vmem_limit_bytes=limit * 1024 * 1024),
        cost_estimate=pl.CostEstimate(flops=flops, bytes_accessed=2**23, transcendentals=0),
        name=name,
    )(scalars, *operands)


def spec_of_cols(wide, col):
    return pl.BlockSpec((1, TILE // 2, wide), lambda i, o: (i, 0, col))


def flat_of(groups):
    counts = [(g[0].shape[0], len(g)) for g in groups]
    return counts, [v for g in groups for v in g]


def first_chunk(scalars, mine, other, groups, width, ck, cot_col):
    counts, flat = flat_of(groups)
    rows = len(CREW) * TILE
    deep = width // len(CHAIN)
    d, *parts = kernel_call(
        lambda *a: first_kernel(*a, counts=counts),
        "first_chunk",
        scalars,
        [mine, other, mine, mine] + flat,
        [
            spec_of_cols(width, 0),
            spec_of_cols(width, 0),
            spec_of_cols(ck, cot_col // ck),
            spec_of_cols(ck, cot_col // ck + 1),
        ]
        + [pl.BlockSpec(memory_space=pltpu.HBM)] * len(flat),
        [pl.BlockSpec((TILE, 2 * ck), lambda i, o: (i, 0))]
        + [pl.BlockSpec((deep, ck), lambda i, o: (0, 0))] * len(CHAIN),
        [jax.ShapeDtypeStruct((rows, 2 * ck), BF)]
        + [jax.ShapeDtypeStruct((deep, ck), BF)] * len(CHAIN),
        [
            pltpu.VMEM((width, 2 * ck), BF),
            pltpu.VMEM((rows, width), BF),
            pltpu.VMEM((rows, ck), BF),
            pltpu.VMEM((width, ck), BF),
            pltpu.SemaphoreType.DMA((DEVS,)),
        ],
        6 * rows * width * ck,
        56,
    )
    return d, parts


def rows_grad(scalars, d, groups, width):
    counts, flat = flat_of(groups)
    rows, wide = d.shape
    gx_spec = pl.BlockSpec((TILE, width // 2), lambda i, o: (i, 0))
    return kernel_call(
        lambda *a: rows_grad_kernel(*a, counts=counts),
        "rows_grad",
        scalars,
        [d] + flat,
        [pl.BlockSpec((TILE, wide), lambda i, o: (i, 0))]
        + [pl.BlockSpec(memory_space=pltpu.HBM)] * len(flat),
        [gx_spec] * 2,
        [jax.ShapeDtypeStruct((rows, width // 2), BF)] * 2,
        [pltpu.VMEM((width, wide), BF), pltpu.SemaphoreType.DMA((DEVS,))],
        2 * rows * width * wide,
        56,
    )


def second_chunk(scalars, mine, other, groups, prev, width, ck, cot_col):
    counts, flat = flat_of(groups)
    rows = len(CREW) * TILE
    gx_spec = pl.BlockSpec((TILE, width // 2), lambda i, o: (i, 0))
    return kernel_call(
        lambda *a: second_kernel(*a, counts=counts),
        "second_chunk",
        scalars,
        [mine, other, mine] + flat + list(prev),
        [
            spec_of_cols(width, 0),
            spec_of_cols(width, 0),
            spec_of_cols(2 * ck, cot_col // (2 * ck)),
        ]
        + [pl.BlockSpec(memory_space=pltpu.HBM)] * len(flat)
        + [gx_spec] * 2,
        [gx_spec] * 2 + [pl.BlockSpec((TILE, ck), lambda i, o: (i, 0))],
        [jax.ShapeDtypeStruct((rows, width // 2), BF)] * 2
        + [jax.ShapeDtypeStruct((rows, ck), BF)],
        [
            pltpu.VMEM((width, 2 * ck), BF),
            pltpu.VMEM((TILE, width), BF),
            pltpu.SemaphoreType.DMA((DEVS,)),
        ],
        8 * rows * width * ck,
        56,
    )


def gate_grad(scalars, mine, other, d, width):
    rows, ck = d.shape
    steps = len(CREW)
    deep = width // steps
    x_spec = pl.BlockSpec((steps, TILE // 2, width // steps), lambda i, o: (0, 0, i))
    return kernel_call(
        gate_grad_kernel,
        "gate_grad",
        scalars,
        [mine, other, d],
        [x_spec, x_spec, pl.BlockSpec((rows, ck), lambda i, o: (0, 0))],
        [pl.BlockSpec((deep, ck), lambda i, o: (0, 0))] * len(CHAIN),
        [jax.ShapeDtypeStruct((deep, ck), BF)] * len(CHAIN),
        [pltpu.VMEM((rows, deep), BF), pltpu.VMEM((width, ck), BF)],
        2 * rows * width * ck,
        56,
    )


def join_kernel(scalars, *refs, quarter):
    out = refs[-1]
    for s in range(len(CREW)):
        start = scalars[DEVS + 2 + s] * quarter
        out[:, pl.ds(pl.multiple_of(start, 128), quarter)] = refs[s][...].astype(F32)


def join_call(scalars, pieces):
    depth, quarter = pieces[0].shape
    vmem = pl.BlockSpec(memory_space=pltpu.VMEM)
    return pl.pallas_call(
        lambda *a: join_kernel(*a, quarter=quarter),
        in_specs=[pl.BlockSpec(memory_space=pltpu.SMEM)] + [vmem] * len(CREW),
        out_specs=vmem,
        out_shape=jax.ShapeDtypeStruct((depth, len(CREW) * quarter), F32),
        compiler_params=pltpu.CompilerParams(vmem_limit_bytes=16 * 1024 * 1024),
        name="join_quarters",
    )(scalars, *pieces)


def split_plan(x_in, cotangent, w_gate, w_up, send_counts, recv_counts):
    rows, width = x_in.shape
    depth, hidden = w_gate.shape
    crew = len(CREW)
    quarter = hidden // crew
    core = lax.axis_index("mp")
    index = lax.axis_index("dp")
    z, place = index // crew, index % crew
    places = [place ^ m for m in CREW]
    chunks = [640, 256]
    offsets = [0, chunks[0]]
    swap = [(0, 1), (1, 0)]

    def columns(array, q, offset, count):
        return lax.dynamic_slice_in_dim(array, q * quarter + offset, count, 1)

    def piece_of_weights(q, k):
        return jnp.concatenate(
            [columns(w, q, offsets[k], chunks[k]) for w in (w_gate, w_up)], axis=1
        )

    order = [z, z ^ 1, jnp.where(z < 2, 2, 1), jnp.where(z < 2, 3, 0)]
    inner = ((z == 1) | (z == 2)).astype(jnp.int32)
    scalars = [index ^ c ^ m for c in CHAIN for m in CREW] + [core, inner] + places
    scalars += [0] * (2 * DEVS - len(scalars)) + [p * crew + q for p in order for q in places]
    scalars = jnp.stack([jnp.asarray(v, jnp.int32) for v in scalars])

    first = [piece_of_weights(q, 0) for q in places]
    own = first[0]
    own_far = send(own, FAR)
    own_near = send(own, NEAR)
    rest = crew_swap(first)[1:]
    own_far, own_near, x_in, cotangent, w_gate, w_up = tie(
        own_far, own_near, x_in, cotangent, w_gate, w_up
    )

    live = jnp.arange(rows) < live_rows_of(send_counts, recv_counts)
    cotangent = jnp.where(live[:, None], cotangent, jnp.zeros((), BF))
    x_half = lax.dynamic_slice_in_dim(x_in, core * (rows // 2), rows // 2, 0)
    parcels = []
    for q in places:
        cot = [columns(cotangent, q, offsets[k], chunks[k]) for k in (1, 0)]
        halves = [c[h : h + rows // 2] for c in cot for h in (0, rows // 2)]
        parcels.append(jnp.concatenate([x_half, *halves, piece_of_weights(q, 1)], axis=1))
    rest = jnp.concatenate(rest, axis=0)
    rest, own_far, *parcels = tie(rest, own_far, *parcels)

    own_both = send(own_far, NEAR)
    rest_far = send(rest, FAR)
    rest_near = send(rest, NEAR)
    parcels = crew_swap(parcels)
    rest_far, rest_near, own_both, *parcels = tie(rest_far, rest_near, own_both, *parcels)

    rest_both = send(rest_far, NEAR)
    mine = jnp.stack(parcels)
    other = lax.ppermute(mine, "mp", swap)
    rest_both, other, mine = tie(rest_both, other, mine)
    second = mine[:, :, width + 2 * quarter :].reshape(crew * depth, 2 * chunks[1])

    cot_second = width
    cot_first = width + 2 * chunks[1]

    second_near = send(second, NEAR)
    second_far = send(second, FAR)
    groups = [(own, own_near, own_far, own_both), (rest, rest_near, rest_far, rest_both)]
    d_first, parts = first_chunk(scalars, mine, other, groups, width, chunks[0], cot_first)
    second_near, second_far, d_first, p0, p1, p2, p3 = tie(second_near, second_far, d_first, *parts)

    middle = along(second, INNER)
    ends = along(second_far, TO_ENDS)
    r1 = along(p3, FROM_ENDS)
    gx = rows_grad(scalars, d_first, groups, width)
    r1, middle, ends, p2, p3, *gx = tie(r1, middle, ends, p2, p3, *gx)
    r2b = along(p2, FROM_ENDS)
    r2a = along(add(p3, r1), INNER)
    keep, give, d_second = second_chunk(
        scalars, mine, other, [(second, second_near, second_far, middle, ends)], gx,
        width, chunks[1], cot_second,
    )
    r2a, r2b, keep, give, d_second = tie(r2a, r2b, keep, give, d_second)

    theirs = lax.ppermute(give, "mp", swap)
    q_parts = gate_grad(scalars, mine, other, d_second, width)
    theirs, *q_parts = tie(theirs, *q_parts)
    q_own, q_near, q_far, q_both = q_parts
    from_near = send(q_both, NEAR)
    r3b = along(add(p2, r2b), INNER)
    r3a = along(add(p1, r2a), OUTER)
    rows_x = crew_swap(
        [
            add(keep[s * rows : (s + 1) * rows], theirs[s * rows : (s + 1) * rows])
            for s in range(crew)
        ]
    )
    sum_far = send(add(q_far, from_near), FAR)
    sum_near = send(q_near, NEAR)
    r3a, r3b, sum_far, sum_near, *rows_x = tie(r3a, r3b, sum_far, sum_near, *rows_x)
    sums = jnp.concatenate([add(p0, r3a, r3b), add(q_own, sum_near, sum_far)], axis=1)
    pieces = crew_swap([sums[s * depth : (s + 1) * depth] for s in range(crew)])
    return add(*rows_x), join_call(scalars, pieces)


def solution(mesh):
    sizes = dict(mesh.shape)
    splits = sizes["dp"] == DEVS and sizes["mp"] == 2
    return jax.shard_map(
        split_plan if splits else general_plan,
        mesh=mesh,
        in_specs=(
            P("dp", None),
            P("dp", "mp"),
            P("dp", "mp"),
            P("dp", "mp"),
            P("dp", None),
            P("dp", None),
        ),
        out_specs=(P("dp", "mp"), P("dp", "mp")),
        check_vma=False,
    )
```

```python
import jax
import jax.numpy as jnp
from jax import lax
from jax.experimental import pallas as pl
from jax.experimental.pallas import tpu as pltpu
from jax.sharding import PartitionSpec as P

BAL = 208
BF = jnp.bfloat16
F32 = jnp.float32


def contract_last(left, right):
    return lax.dot_general(
        left, right, (((1,), (1,)), ((), ())), preferred_element_type=F32
    )


def contract_first(left, right):
    return lax.dot_general(
        left, right, (((0,), (0,)), ((), ())), preferred_element_type=F32
    )


def swiglu_back(x_rows, cot_rows, gate_full, up_full, live_mask):
    gate_val = jnp.dot(x_rows, gate_full, preferred_element_type=F32)
    up_val = jnp.dot(x_rows, up_full, preferred_element_type=F32)
    sig = jax.nn.sigmoid(gate_val)
    cot_val = cot_rows.astype(F32)
    d_gate = jnp.where(
        live_mask[:, None], cot_val * up_val * sig * (1.0 + gate_val * (1.0 - sig)), 0.0
    ).astype(BF)
    d_up = jnp.where(live_mask[:, None], cot_val * gate_val * sig, 0.0).astype(BF)
    return contract_last(d_gate, gate_full) + contract_last(d_up, up_full), d_gate


def live_rows_of(send_counts, recv_counts):
    return BAL + jnp.sum(send_counts[0]) - jnp.sum(recv_counts[0])


def general_plan(x_in, cotangent, w_gate, w_up, send_counts, recv_counts):
    dev_count = lax.axis_size("dp")
    gate_full = lax.all_gather(w_gate, "dp", axis=0, tiled=True)
    up_full = lax.all_gather(w_up, "dp", axis=0, tiled=True)
    live_mask = jnp.arange(x_in.shape[0]) < live_rows_of(send_counts, recv_counts)
    partial_value, d_gate = swiglu_back(x_in, cotangent, gate_full, up_full, live_mask)
    grad_x = lax.psum_scatter(
        partial_value.astype(BF), "mp", scatter_dimension=1, tiled=True
    )
    whole = contract_first(x_in, d_gate)
    pieces = lax.all_to_all(
        whole.reshape(dev_count, x_in.shape[1] // dev_count, whole.shape[1]),
        "dp",
        split_axis=0,
        concat_axis=0,
        tiled=True,
    )
    return grad_x, jnp.sum(pieces, axis=0)


CREW = (0, 1, 2, 3)
NEAR, FAR = 4, 8
CHAIN = (0, NEAR, FAR, NEAR | FAR)
DEVS = 16
TILE = 256


def tie(*values):
    return lax.optimization_barrier(values)


def send(value, mask):
    return lax.ppermute(value, "dp", [(i, i ^ mask) for i in range(DEVS)])


def along(value, moves):
    crew = len(CREW)
    return lax.ppermute(
        value, "dp", [(crew * a + q, crew * b + q) for a, b in moves for q in range(crew)]
    )


OUTER = [(0, 1), (1, 0), (2, 3), (3, 2)]
INNER = [(1, 2), (2, 1)]
TO_ENDS = [(1, 0), (2, 3)]
FROM_ENDS = [(0, 1), (3, 2)]


def crew_swap(pieces):
    return [send(p, m) if m else p for p, m in zip(pieces, CREW)]


def add(*terms):
    total = terms[0].astype(F32)
    for term in terms[1:]:
        total = total + term.astype(F32)
    return total.astype(BF)


def place_weights(scalars, groups, w_all, sems, act):
    blk = w_all.shape[0] // DEVS
    crew = len(CREW)
    inner = scalars[DEVS + 1]
    base = 0
    for n, members in groups:
        for c, member in enumerate(members):
            for i in range(n // blk):
                j = min(c, len(CHAIN) - 1) * crew + base + i
                start = pl.multiple_of(scalars[j] * blk, blk)
                copy = pltpu.make_async_copy(
                    member.at[pl.ds(i * blk, blk), :], w_all.at[pl.ds(start, blk), :], sems.at[j]
                )
                if len(members) > len(CHAIN) and c >= len(CHAIN) - 1:
                    pl.when(inner == (1 if c == len(CHAIN) - 1 else 0))(
                        lambda copy=copy: act(copy)
                    )
                else:
                    act(copy)
        base += n // blk


def grouped(refs, counts):
    groups = []
    for n, members in counts:
        groups.append((n, refs[:members]))
        refs = refs[members:]
    return groups, refs


def place_rows(core, tile, mine_ref, other_ref, cols=slice(None)):
    rows = TILE // 2
    lower = pl.ds(pl.multiple_of(core * rows, rows), rows)
    upper = pl.ds(pl.multiple_of((1 - core) * rows, rows), rows)
    tile[lower, :] = mine_ref[0, :, cols]
    tile[upper, :] = other_ref[0, :, cols]


def store_rows_grad(core, gx, gx_refs, prev):
    half = gx.shape[1] // 2
    low, high = gx[:, :half], gx[:, half:]
    for keep in range(2):

        @pl.when(core == keep)
        def _():
            for i, value in enumerate(((low, high)[keep], (high, low)[keep])):
                if prev is not None:
                    value = value + prev[i][...].astype(F32)
                gx_refs[i][...] = value.astype(BF)


def front(x, w_all, cot_lower, cot_upper):
    ck = w_all.shape[1] // 2
    both = jnp.dot(x, w_all[...], preferred_element_type=F32)
    gate, up = both[:, :ck], both[:, ck:]
    cot = jnp.concatenate([cot_lower, cot_upper], axis=0).astype(F32)
    sig = jax.nn.sigmoid(gate)
    d_gate = (cot * up * sig * (1.0 + gate * (1.0 - sig))).astype(BF)
    d_up = (cot * gate * sig).astype(BF)
    return d_gate, d_up


def pack_kernel(scalars, sent, got, x_ref, cot_ref, gate_ref, up_ref, *outs, chunks, quarter):
    rows, width = x_ref.shape
    half = rows // 2
    live = BAL
    for i in range(sent.shape[1]):
        live = live + sent[0, i] - got[0, i]
    is_live = lax.broadcasted_iota(jnp.int32, (rows, 1), 0) < live
    x_half = x_ref[pl.ds(pl.multiple_of(scalars[DEVS] * half, half), half), :]
    for s, out in enumerate(outs):
        start = scalars[DEVS + 2 + s] * quarter
        out[:, :width] = x_half
        col = width
        for k in (1, 0):
            spot = pl.ds(pl.multiple_of(start + sum(chunks[:k]), 128), chunks[k])
            cot = jnp.where(is_live, cot_ref[:, spot].astype(F32), 0.0).astype(BF)
            for part in (cot[:half], cot[half:]):
                out[:, col : col + chunks[k]] = part
                col += chunks[k]
        spot = pl.ds(pl.multiple_of(start + chunks[0], 128), chunks[1])
        for ref in (gate_ref, up_ref):
            out[:, col : col + chunks[1]] = ref[:, spot]
            col += chunks[1]


def pack_parcels(scalars, sent, got, x_in, cotangent, w_gate, w_up, chunks):
    rows, width = x_in.shape
    quarter = sum(chunks)
    vmem = pl.BlockSpec(memory_space=pltpu.VMEM)
    smem = pl.BlockSpec(memory_space=pltpu.SMEM)
    wide = width + 2 * quarter + 2 * chunks[1]
    return pl.pallas_call(
        lambda *a: pack_kernel(*a, chunks=chunks, quarter=quarter),
        in_specs=[smem] * 3 + [vmem] * 4,
        out_specs=[vmem] * len(CREW),
        out_shape=[jax.ShapeDtypeStruct((rows // 2, wide), BF)] * len(CREW),
        compiler_params=pltpu.CompilerParams(vmem_limit_bytes=32 * 1024 * 1024),
        cost_estimate=pl.CostEstimate(flops=0, bytes_accessed=2**23, transcendentals=0),
        name="pack_parcels",
    )(scalars, sent, got, x_in, cotangent, w_gate, w_up)


def first_kernel(scalars, mine_ref, other_ref, low_ref, high_ref, *refs, counts):
    groups, refs = grouped(refs, counts)
    d_ref, refs = refs[0], refs[1:]
    gg_refs, (w_all, x_all, d_all, acc, sems) = refs[: len(CHAIN)], refs[len(CHAIN) :]
    step = pl.program_id(0)
    width = w_all.shape[0]
    blk = width // DEVS
    crew = len(CREW)

    @pl.when(step == 0)
    def _():
        place_weights(scalars, groups, w_all, sems, lambda copy: copy.start())

    here = pl.ds(pl.multiple_of(step * TILE, TILE), TILE)
    place_rows(scalars[DEVS], x_all.at[here], mine_ref, other_ref)

    @pl.when(step == 0)
    def _():
        place_weights(scalars, groups, w_all, sems, lambda copy: copy.wait())

    d_gate, d_up = front(x_all[here, :], w_all, low_ref[0], high_ref[0])
    d_all[here, :] = d_gate
    d_ref[...] = jnp.concatenate([d_gate, d_up], axis=1)

    @pl.when(step == pl.num_programs(0) - 1)
    def _():
        d = d_all[...]
        deep = crew * blk
        for r in range(len(CHAIN)):
            cols = slice(r * deep, (r + 1) * deep)
            acc[cols, :] = contract_first(x_all[:, cols], d).astype(BF)
        for j in range(DEVS):
            row = (j % crew) * blk
            at_row = pl.multiple_of(scalars[2 * DEVS + j] * blk, blk)
            gg_refs[j // crew][row : row + blk, :] = acc[pl.ds(at_row, blk), :]


def rows_grad_kernel(scalars, d_ref, *refs, counts):
    groups, refs = grouped(refs, counts)
    gx_refs, (w_all, sems) = refs[:2], refs[2:]

    @pl.when(pl.program_id(0) == 0)
    def _():
        place_weights(scalars, groups, w_all, sems, lambda copy: copy.start())
        place_weights(scalars, groups, w_all, sems, lambda copy: copy.wait())

    store_rows_grad(scalars[DEVS], contract_last(d_ref[...], w_all[...]), gx_refs, None)


def second_kernel(scalars, mine_ref, other_ref, cot_ref, *refs, counts):
    groups, refs = grouped(refs, counts)
    prev, gx_refs, (d_ref, w_all, x_tile, sems) = refs[:2], refs[2:4], refs[4:]
    step = pl.program_id(0)
    ck = d_ref.shape[1]

    @pl.when(step == 0)
    def _():
        place_weights(scalars, groups, w_all, sems, lambda copy: copy.start())

    place_rows(scalars[DEVS], x_tile, mine_ref, other_ref)

    @pl.when(step == 0)
    def _():
        place_weights(scalars, groups, w_all, sems, lambda copy: copy.wait())

    d_gate, d_up = front(x_tile[...], w_all, cot_ref[0, :, :ck], cot_ref[0, :, ck:])
    d_ref[...] = d_gate
    gx = contract_last(jnp.concatenate([d_gate, d_up], axis=1), w_all[...])
    store_rows_grad(scalars[DEVS], gx, gx_refs, prev)


def gate_grad_kernel(scalars, mine_ref, other_ref, d_ref, *refs):
    out_refs, (x_all, acc) = refs[: len(CHAIN)], refs[len(CHAIN) :]
    step = pl.program_id(0)
    core = scalars[DEVS]
    crew = len(CREW)
    for s in range(crew):
        tile = x_all.at[s * TILE : (s + 1) * TILE]
        place_rows(core, tile, mine_ref.at[s : s + 1], other_ref.at[s : s + 1])
    deep = x_all.shape[1]
    here = pl.ds(pl.multiple_of(step * deep, deep), deep)
    acc[here, :] = contract_first(x_all[...], d_ref[...]).astype(BF)

    @pl.when(step == pl.num_programs(0) - 1)
    def _():
        blk = deep // crew
        for j in range(DEVS):
            row = (j % crew) * blk
            at_row = pl.multiple_of(scalars[j] * blk, blk)
            out_refs[j // crew][row : row + blk, :] = acc[pl.ds(at_row, blk), :]


def kernel_call(body, name, scalars, operands, in_specs, out_specs, out_shape, scratch, flops, limit):
    return pl.pallas_call(
        body,
        grid_spec=pltpu.PrefetchScalarGridSpec(
            num_scalar_prefetch=1,
            grid=(len(CREW),),
            in_specs=in_specs,
            out_specs=out_specs,
            scratch_shapes=scratch,
        ),
        out_shape=out_shape,
        compiler_params=pltpu.CompilerParams(vmem_limit_bytes=limit * 1024 * 1024),
        cost_estimate=pl.CostEstimate(flops=flops, bytes_accessed=2**23, transcendentals=0),
        name=name,
    )(scalars, *operands)


def spec_of_cols(wide, col):
    return pl.BlockSpec((1, TILE // 2, wide), lambda i, o: (i, 0, col))


def flat_of(groups):
    counts = [(g[0].shape[0], len(g)) for g in groups]
    return counts, [v for g in groups for v in g]


def first_chunk(scalars, mine, other, groups, width, ck, cot_col):
    counts, flat = flat_of(groups)
    rows = len(CREW) * TILE
    deep = width // len(CHAIN)
    d, *parts = kernel_call(
        lambda *a: first_kernel(*a, counts=counts),
        "first_chunk",
        scalars,
        [mine, other, mine, mine] + flat,
        [
            spec_of_cols(width, 0),
            spec_of_cols(width, 0),
            spec_of_cols(ck, cot_col // ck),
            spec_of_cols(ck, cot_col // ck + 1),
        ]
        + [pl.BlockSpec(memory_space=pltpu.HBM)] * len(flat),
        [pl.BlockSpec((TILE, 2 * ck), lambda i, o: (i, 0))]
        + [pl.BlockSpec((deep, ck), lambda i, o: (0, 0))] * len(CHAIN),
        [jax.ShapeDtypeStruct((rows, 2 * ck), BF)]
        + [jax.ShapeDtypeStruct((deep, ck), BF)] * len(CHAIN),
        [
            pltpu.VMEM((width, 2 * ck), BF),
            pltpu.VMEM((rows, width), BF),
            pltpu.VMEM((rows, ck), BF),
            pltpu.VMEM((width, ck), BF),
            pltpu.SemaphoreType.DMA((DEVS,)),
        ],
        6 * rows * width * ck,
        32,
    )
    return d, parts


def rows_grad(scalars, d, groups, width):
    counts, flat = flat_of(groups)
    rows, wide = d.shape
    gx_spec = pl.BlockSpec((TILE, width // 2), lambda i, o: (i, 0))
    return kernel_call(
        lambda *a: rows_grad_kernel(*a, counts=counts),
        "rows_grad",
        scalars,
        [d] + flat,
        [pl.BlockSpec((TILE, wide), lambda i, o: (i, 0))]
        + [pl.BlockSpec(memory_space=pltpu.HBM)] * len(flat),
        [gx_spec] * 2,
        [jax.ShapeDtypeStruct((rows, width // 2), BF)] * 2,
        [pltpu.VMEM((width, wide), BF), pltpu.SemaphoreType.DMA((DEVS,))],
        2 * rows * width * wide,
        24,
    )


def second_chunk(scalars, mine, other, groups, prev, width, ck, cot_col):
    counts, flat = flat_of(groups)
    rows = len(CREW) * TILE
    gx_spec = pl.BlockSpec((TILE, width // 2), lambda i, o: (i, 0))
    return kernel_call(
        lambda *a: second_kernel(*a, counts=counts),
        "second_chunk",
        scalars,
        [mine, other, mine] + flat + list(prev),
        [
            spec_of_cols(width, 0),
            spec_of_cols(width, 0),
            spec_of_cols(2 * ck, cot_col // (2 * ck)),
        ]
        + [pl.BlockSpec(memory_space=pltpu.HBM)] * len(flat)
        + [gx_spec] * 2,
        [gx_spec] * 2 + [pl.BlockSpec((TILE, ck), lambda i, o: (i, 0))],
        [jax.ShapeDtypeStruct((rows, width // 2), BF)] * 2
        + [jax.ShapeDtypeStruct((rows, ck), BF)],
        [
            pltpu.VMEM((width, 2 * ck), BF),
            pltpu.VMEM((TILE, width), BF),
            pltpu.SemaphoreType.DMA((DEVS,)),
        ],
        8 * rows * width * ck,
        24,
    )


def gate_grad(scalars, mine, other, d, width):
    rows, ck = d.shape
    steps = len(CREW)
    deep = width // steps
    x_spec = pl.BlockSpec((steps, TILE // 2, width // steps), lambda i, o: (0, 0, i))
    return kernel_call(
        gate_grad_kernel,
        "gate_grad",
        scalars,
        [mine, other, d],
        [x_spec, x_spec, pl.BlockSpec((rows, ck), lambda i, o: (0, 0))],
        [pl.BlockSpec((deep, ck), lambda i, o: (0, 0))] * len(CHAIN),
        [jax.ShapeDtypeStruct((deep, ck), BF)] * len(CHAIN),
        [pltpu.VMEM((rows, deep), BF), pltpu.VMEM((width, ck), BF)],
        2 * rows * width * ck,
        24,
    )


def join_kernel(scalars, *refs, quarter):
    out = refs[-1]
    for i, ref in enumerate(refs[:-1]):
        ck = ref.shape[1]
        start = scalars[DEVS + 2 + i % len(CREW)] * quarter
        if i >= len(CREW):
            start = start + refs[0].shape[1]
        out[:, pl.ds(pl.multiple_of(start, 128), ck)] = ref[...].astype(F32)


def join_call(scalars, pieces):
    depth = pieces[0].shape[0]
    quarter = pieces[0].shape[1] + pieces[-1].shape[1]
    vmem = pl.BlockSpec(memory_space=pltpu.VMEM)
    return pl.pallas_call(
        lambda *a: join_kernel(*a, quarter=quarter),
        in_specs=[pl.BlockSpec(memory_space=pltpu.SMEM)] + [vmem] * len(pieces),
        out_specs=vmem,
        out_shape=jax.ShapeDtypeStruct((depth, len(CREW) * quarter), F32),
        compiler_params=pltpu.CompilerParams(vmem_limit_bytes=16 * 1024 * 1024),
        name="join_quarters",
    )(scalars, *pieces)


def split_plan(x_in, cotangent, w_gate, w_up, send_counts, recv_counts):
    rows, width = x_in.shape
    depth, hidden = w_gate.shape
    crew = len(CREW)
    quarter = hidden // crew
    core = lax.axis_index("mp")
    index = lax.axis_index("dp")
    z, place = index // crew, index % crew
    places = [place ^ m for m in CREW]
    chunks = [640, 256]
    offsets = [0, chunks[0]]
    swap = [(0, 1), (1, 0)]

    def columns(array, q, offset, count):
        return lax.dynamic_slice_in_dim(array, q * quarter + offset, count, 1)

    def piece_of_weights(q, k):
        return jnp.concatenate(
            [columns(w, q, offsets[k], chunks[k]) for w in (w_gate, w_up)], axis=1
        )

    order = [z, z ^ 1, jnp.where(z < 2, 2, 1), jnp.where(z < 2, 3, 0)]
    inner = ((z == 1) | (z == 2)).astype(jnp.int32)
    scalars = [index ^ c ^ m for c in CHAIN for m in CREW] + [core, inner] + places
    scalars += [0] * (2 * DEVS - len(scalars)) + [p * crew + q for p in order for q in places]
    scalars = jnp.stack([jnp.asarray(v, jnp.int32) for v in scalars])

    first = [piece_of_weights(q, 0) for q in places]
    own = first[0]
    own_far = send(own, FAR)
    own_near = send(own, NEAR)
    rest = crew_swap(first)[1:]
    own_far, own_near, x_in, cotangent, w_gate, w_up = tie(
        own_far, own_near, x_in, cotangent, w_gate, w_up
    )
    parcels = pack_parcels(
        scalars, send_counts, recv_counts, x_in, cotangent, w_gate, w_up, chunks
    )
    rest = jnp.concatenate(rest, axis=0)
    rest, own_far, *parcels = tie(rest, own_far, *parcels)

    own_both = send(own_far, NEAR)
    rest_far = send(rest, FAR)
    rest_near = send(rest, NEAR)
    parcels = crew_swap(parcels)
    rest_far, rest_near, own_both, *parcels = tie(rest_far, rest_near, own_both, *parcels)

    rest_both = send(rest_far, NEAR)
    mine = jnp.stack(parcels)
    other = lax.ppermute(mine, "mp", swap)
    second = mine[:, :, width + 2 * quarter :].reshape(crew * depth, 2 * chunks[1])
    rest_both, other, second = tie(rest_both, other, second)

    cot_second = width
    cot_first = width + 2 * chunks[1]

    second_near = send(second, NEAR)
    second_far = send(second, FAR)
    groups = [(own, own_near, own_far, own_both), (rest, rest_near, rest_far, rest_both)]
    d_first, parts = first_chunk(scalars, mine, other, groups, width, chunks[0], cot_first)
    second_near, second_far, d_first, p0, p1, p2, p3 = tie(second_near, second_far, d_first, *parts)

    middle = along(second, INNER)
    ends = along(second_far, TO_ENDS)
    r1 = along(p3, FROM_ENDS)
    gx = rows_grad(scalars, d_first, groups, width)
    r1, middle, ends, p2, p3, *gx = tie(r1, middle, ends, p2, p3, *gx)
    r2b = along(p2, FROM_ENDS)
    r2a = along(add(p3, r1), INNER)
    keep, give, d_second = second_chunk(
        scalars, mine, other, [(second, second_near, second_far, middle, ends)], gx,
        width, chunks[1], cot_second,
    )
    r2a, r2b, keep, give, d_second = tie(r2a, r2b, keep, give, d_second)

    theirs = lax.ppermute(give, "mp", swap)
    q_parts = gate_grad(scalars, mine, other, d_second, width)
    theirs, *q_parts = tie(theirs, *q_parts)
    q_own, q_near, q_far, q_both = q_parts
    from_near = send(q_both, NEAR)
    r3b = along(add(p2, r2b), INNER)
    r3a = along(add(p1, r2a), OUTER)
    rows_x = crew_swap(
        [
            add(keep[s * rows : (s + 1) * rows], theirs[s * rows : (s + 1) * rows])
            for s in range(crew)
        ]
    )
    from_near, r3a, r3b = tie(from_near, r3a, r3b)
    sum_far = send(add(q_far, from_near), FAR)
    sum_near = send(q_near, NEAR)
    sums = add(p0, r3a, r3b)
    firsts = crew_swap([sums[s * depth : (s + 1) * depth] for s in range(crew)])
    sum_far, sum_near, *rows_x = tie(sum_far, sum_near, *rows_x)
    sums = add(q_own, sum_near, sum_far)
    lasts = crew_swap([sums[s * depth : (s + 1) * depth] for s in range(crew)])
    return add(*rows_x), join_call(scalars, firsts + lasts)


def solution(mesh):
    sizes = dict(mesh.shape)
    splits = sizes["dp"] == DEVS and sizes["mp"] == 2
    return jax.shard_map(
        split_plan if splits else general_plan,
        mesh=mesh,
        in_specs=(
            P("dp", None),
            P("dp", "mp"),
            P("dp", "mp"),
            P("dp", "mp"),
            P("dp", None),
            P("dp", None),
        ),
        out_specs=(P("dp", "mp"), P("dp", "mp")),
        check_vma=False,
    )
```

```python
import jax
import jax.numpy as jnp
from jax import lax
from jax.experimental import pallas as pl
from jax.experimental.pallas import tpu as pltpu
from jax.sharding import PartitionSpec as P

BAL = 208
BF = jnp.bfloat16
F32 = jnp.float32


def contract_last(left, right):
    return lax.dot_general(
        left, right, (((1,), (1,)), ((), ())), preferred_element_type=F32
    )


def contract_first(left, right):
    return lax.dot_general(
        left, right, (((0,), (0,)), ((), ())), preferred_element_type=F32
    )


def swiglu_back(x_rows, cot_rows, gate_full, up_full, live_mask):
    gate_val = jnp.dot(x_rows, gate_full, preferred_element_type=F32)
    up_val = jnp.dot(x_rows, up_full, preferred_element_type=F32)
    sig = jax.nn.sigmoid(gate_val)
    cot_val = cot_rows.astype(F32)
    d_gate = jnp.where(
        live_mask[:, None], cot_val * up_val * sig * (1.0 + gate_val * (1.0 - sig)), 0.0
    ).astype(BF)
    d_up = jnp.where(live_mask[:, None], cot_val * gate_val * sig, 0.0).astype(BF)
    return contract_last(d_gate, gate_full) + contract_last(d_up, up_full), d_gate


def live_rows_of(send_counts, recv_counts):
    return BAL + jnp.sum(send_counts[0]) - jnp.sum(recv_counts[0])


def general_plan(x_in, cotangent, w_gate, w_up, send_counts, recv_counts):
    dev_count = lax.axis_size("dp")
    gate_full = lax.all_gather(w_gate, "dp", axis=0, tiled=True)
    up_full = lax.all_gather(w_up, "dp", axis=0, tiled=True)
    live_mask = jnp.arange(x_in.shape[0]) < live_rows_of(send_counts, recv_counts)
    partial_value, d_gate = swiglu_back(x_in, cotangent, gate_full, up_full, live_mask)
    grad_x = lax.psum_scatter(
        partial_value.astype(BF), "mp", scatter_dimension=1, tiled=True
    )
    whole = contract_first(x_in, d_gate)
    pieces = lax.all_to_all(
        whole.reshape(dev_count, x_in.shape[1] // dev_count, whole.shape[1]),
        "dp",
        split_axis=0,
        concat_axis=0,
        tiled=True,
    )
    return grad_x, jnp.sum(pieces, axis=0)


CREW = (0, 1, 2, 3)
NEAR, FAR = 4, 8
CHAIN = (0, NEAR, FAR, NEAR | FAR)
DEVS = 16
TILE = 256


def tie(*values):
    return lax.optimization_barrier(values)


def send(value, mask):
    return lax.ppermute(value, "dp", [(i, i ^ mask) for i in range(DEVS)])


def along(value, moves):
    crew = len(CREW)
    return lax.ppermute(
        value, "dp", [(crew * a + q, crew * b + q) for a, b in moves for q in range(crew)]
    )


OUTER = [(0, 1), (1, 0), (2, 3), (3, 2)]
INNER = [(1, 2), (2, 1)]
TO_ENDS = [(1, 0), (2, 3)]
FROM_ENDS = [(0, 1), (3, 2)]


def crew_swap(pieces):
    return [send(p, m) if m else p for p, m in zip(pieces, CREW)]


def add(*terms):
    total = terms[0].astype(F32)
    for term in terms[1:]:
        total = total + term.astype(F32)
    return total.astype(BF)


def place_weights(scalars, groups, w_all, sems, act):
    blk = w_all.shape[0] // DEVS
    crew = len(CREW)
    inner = scalars[DEVS + 1]
    base = 0
    for n, members in groups:
        for c, member in enumerate(members):
            for i in range(n // blk):
                j = min(c, len(CHAIN) - 1) * crew + base + i
                start = pl.multiple_of(scalars[j] * blk, blk)
                copy = pltpu.make_async_copy(
                    member.at[pl.ds(i * blk, blk), :], w_all.at[pl.ds(start, blk), :], sems.at[j]
                )
                if len(members) > len(CHAIN) and c >= len(CHAIN) - 1:
                    pl.when(inner == (1 if c == len(CHAIN) - 1 else 0))(
                        lambda copy=copy: act(copy)
                    )
                else:
                    act(copy)
        base += n // blk


def grouped(refs, counts):
    groups = []
    for n, members in counts:
        groups.append((n, refs[:members]))
        refs = refs[members:]
    return groups, refs


def place_rows(core, tile, mine_ref, other_ref, cols=slice(None)):
    rows = TILE // 2
    lower = pl.ds(pl.multiple_of(core * rows, rows), rows)
    upper = pl.ds(pl.multiple_of((1 - core) * rows, rows), rows)
    tile[lower, :] = mine_ref[0, :, cols]
    tile[upper, :] = other_ref[0, :, cols]


def store_rows_grad(core, gx, gx_refs, prev):
    half = gx.shape[1] // 2
    low, high = gx[:, :half], gx[:, half:]
    for keep in range(2):

        @pl.when(core == keep)
        def _():
            for i, value in enumerate(((low, high)[keep], (high, low)[keep])):
                if prev is not None:
                    value = value + prev[i][...].astype(F32)
                gx_refs[i][...] = value.astype(BF)


def front(x, w_all, cot_lower, cot_upper):
    ck = w_all.shape[1] // 2
    both = jnp.dot(x, w_all[...], preferred_element_type=F32)
    gate, up = both[:, :ck], both[:, ck:]
    cot = jnp.concatenate([cot_lower, cot_upper], axis=0).astype(F32)
    sig = jax.nn.sigmoid(gate)
    d_gate = (cot * up * sig * (1.0 + gate * (1.0 - sig))).astype(BF)
    d_up = (cot * gate * sig).astype(BF)
    return d_gate, d_up


def pack_kernel(scalars, sent, got, x_ref, cot_ref, gate_ref, up_ref, *outs, chunks, quarter):
    rows, width = x_ref.shape
    half = rows // 2
    live = BAL
    for i in range(sent.shape[1]):
        live = live + sent[0, i] - got[0, i]
    is_live = lax.broadcasted_iota(jnp.int32, (rows, 1), 0) < live
    x_half = x_ref[pl.ds(pl.multiple_of(scalars[DEVS] * half, half), half), :]
    for s, out in enumerate(outs):
        start = scalars[DEVS + 2 + s] * quarter
        out[:, :width] = x_half
        col = width
        for k in (1, 0):
            spot = pl.ds(pl.multiple_of(start + sum(chunks[:k]), 128), chunks[k])
            cot = jnp.where(is_live, cot_ref[:, spot].astype(F32), 0.0).astype(BF)
            for part in (cot[:half], cot[half:]):
                out[:, col : col + chunks[k]] = part
                col += chunks[k]
        spot = pl.ds(pl.multiple_of(start + chunks[0], 128), chunks[1])
        for ref in (gate_ref, up_ref):
            out[:, col : col + chunks[1]] = ref[:, spot]
            col += chunks[1]


def pack_parcels(scalars, sent, got, x_in, cotangent, w_gate, w_up, chunks):
    rows, width = x_in.shape
    quarter = sum(chunks)
    vmem = pl.BlockSpec(memory_space=pltpu.VMEM)
    smem = pl.BlockSpec(memory_space=pltpu.SMEM)
    wide = width + 2 * quarter + 2 * chunks[1]
    return pl.pallas_call(
        lambda *a: pack_kernel(*a, chunks=chunks, quarter=quarter),
        in_specs=[smem] * 3 + [vmem] * 4,
        out_specs=[vmem] * len(CREW),
        out_shape=[jax.ShapeDtypeStruct((rows // 2, wide), BF)] * len(CREW),
        compiler_params=pltpu.CompilerParams(vmem_limit_bytes=32 * 1024 * 1024),
        cost_estimate=pl.CostEstimate(flops=0, bytes_accessed=2**23, transcendentals=0),
        name="pack_parcels",
    )(scalars, sent, got, x_in, cotangent, w_gate, w_up)


def first_kernel(scalars, mine_ref, other_ref, low_ref, high_ref, *refs, counts):
    groups, refs = grouped(refs, counts)
    d_ref, refs = refs[0], refs[1:]
    gg_refs, (w_all, x_all, d_all, acc, sems) = refs[: len(CHAIN)], refs[len(CHAIN) :]
    step = pl.program_id(0)
    width = w_all.shape[0]
    blk = width // DEVS
    crew = len(CREW)

    @pl.when(step == 0)
    def _():
        place_weights(scalars, groups, w_all, sems, lambda copy: copy.start())

    here = pl.ds(pl.multiple_of(step * TILE, TILE), TILE)
    place_rows(scalars[DEVS], x_all.at[here], mine_ref, other_ref)

    @pl.when(step == 0)
    def _():
        place_weights(scalars, groups, w_all, sems, lambda copy: copy.wait())

    d_gate, d_up = front(x_all[here, :], w_all, low_ref[0], high_ref[0])
    d_all[here, :] = d_gate
    d_ref[...] = jnp.concatenate([d_gate, d_up], axis=1)

    @pl.when(step == pl.num_programs(0) - 1)
    def _():
        d = d_all[...]
        deep = crew * blk
        for r in range(len(CHAIN)):
            cols = slice(r * deep, (r + 1) * deep)
            acc[cols, :] = contract_first(x_all[:, cols], d).astype(BF)
        for j in range(DEVS):
            row = (j % crew) * blk
            at_row = pl.multiple_of(scalars[2 * DEVS + j] * blk, blk)
            gg_refs[j // crew][row : row + blk, :] = acc[pl.ds(at_row, blk), :]


def rows_grad_kernel(scalars, d_ref, *refs, counts):
    groups, refs = grouped(refs, counts)
    gx_refs, (w_all, sems) = refs[:2], refs[2:]

    @pl.when(pl.program_id(0) == 0)
    def _():
        place_weights(scalars, groups, w_all, sems, lambda copy: copy.start())
        place_weights(scalars, groups, w_all, sems, lambda copy: copy.wait())

    store_rows_grad(scalars[DEVS], contract_last(d_ref[...], w_all[...]), gx_refs, None)


def second_kernel(scalars, mine_ref, other_ref, cot_ref, *refs, counts):
    groups, refs = grouped(refs, counts)
    prev, gx_refs, (d_ref, w_all, x_tile, sems) = refs[:2], refs[2:4], refs[4:]
    step = pl.program_id(0)
    ck = d_ref.shape[1]

    @pl.when(step == 0)
    def _():
        place_weights(scalars, groups, w_all, sems, lambda copy: copy.start())

    place_rows(scalars[DEVS], x_tile, mine_ref, other_ref)

    @pl.when(step == 0)
    def _():
        place_weights(scalars, groups, w_all, sems, lambda copy: copy.wait())

    d_gate, d_up = front(x_tile[...], w_all, cot_ref[0, :, :ck], cot_ref[0, :, ck:])
    d_ref[...] = d_gate
    gx = contract_last(jnp.concatenate([d_gate, d_up], axis=1), w_all[...])
    store_rows_grad(scalars[DEVS], gx, gx_refs, prev)


def gate_grad_kernel(scalars, mine_ref, other_ref, d_ref, *refs):
    out_refs, (x_all, acc) = refs[: len(CHAIN)], refs[len(CHAIN) :]
    step = pl.program_id(0)
    core = scalars[DEVS]
    crew = len(CREW)
    for s in range(crew):
        tile = x_all.at[s * TILE : (s + 1) * TILE]
        place_rows(core, tile, mine_ref.at[s : s + 1], other_ref.at[s : s + 1])
    deep = x_all.shape[1]
    here = pl.ds(pl.multiple_of(step * deep, deep), deep)
    acc[here, :] = contract_first(x_all[...], d_ref[...]).astype(BF)

    @pl.when(step == pl.num_programs(0) - 1)
    def _():
        blk = deep // crew
        for j in range(DEVS):
            row = (j % crew) * blk
            at_row = pl.multiple_of(scalars[j] * blk, blk)
            out_refs[j // crew][row : row + blk, :] = acc[pl.ds(at_row, blk), :]


def kernel_call(body, name, scalars, operands, in_specs, out_specs, out_shape, scratch, flops, limit):
    return pl.pallas_call(
        body,
        grid_spec=pltpu.PrefetchScalarGridSpec(
            num_scalar_prefetch=1,
            grid=(len(CREW),),
            in_specs=in_specs,
            out_specs=out_specs,
            scratch_shapes=scratch,
        ),
        out_shape=out_shape,
        compiler_params=pltpu.CompilerParams(vmem_limit_bytes=limit * 1024 * 1024),
        cost_estimate=pl.CostEstimate(flops=flops, bytes_accessed=2**23, transcendentals=0),
        name=name,
    )(scalars, *operands)


def spec_of_cols(wide, col):
    return pl.BlockSpec((1, TILE // 2, wide), lambda i, o: (i, 0, col))


def flat_of(groups):
    counts = [(g[0].shape[0], len(g)) for g in groups]
    return counts, [v for g in groups for v in g]


def first_chunk(scalars, mine, other, groups, width, ck, cot_col):
    counts, flat = flat_of(groups)
    rows = len(CREW) * TILE
    deep = width // len(CHAIN)
    d, *parts = kernel_call(
        lambda *a: first_kernel(*a, counts=counts),
        "first_chunk",
        scalars,
        [mine, other, mine, mine] + flat,
        [
            spec_of_cols(width, 0),
            spec_of_cols(width, 0),
            spec_of_cols(ck, cot_col // ck),
            spec_of_cols(ck, cot_col // ck + 1),
        ]
        + [pl.BlockSpec(memory_space=pltpu.HBM)] * len(flat),
        [pl.BlockSpec((TILE, 2 * ck), lambda i, o: (i, 0))]
        + [pl.BlockSpec((deep, ck), lambda i, o: (0, 0))] * len(CHAIN),
        [jax.ShapeDtypeStruct((rows, 2 * ck), BF)]
        + [jax.ShapeDtypeStruct((deep, ck), BF)] * len(CHAIN),
        [
            pltpu.VMEM((width, 2 * ck), BF),
            pltpu.VMEM((rows, width), BF),
            pltpu.VMEM((rows, ck), BF),
            pltpu.VMEM((width, ck), BF),
            pltpu.SemaphoreType.DMA((DEVS,)),
        ],
        6 * rows * width * ck,
        32,
    )
    return d, parts


def rows_grad(scalars, d, groups, width):
    counts, flat = flat_of(groups)
    rows, wide = d.shape
    gx_spec = pl.BlockSpec((TILE, width // 2), lambda i, o: (i, 0))
    return kernel_call(
        lambda *a: rows_grad_kernel(*a, counts=counts),
        "rows_grad",
        scalars,
        [d] + flat,
        [pl.BlockSpec((TILE, wide), lambda i, o: (i, 0))]
        + [pl.BlockSpec(memory_space=pltpu.HBM)] * len(flat),
        [gx_spec] * 2,
        [jax.ShapeDtypeStruct((rows, width // 2), BF)] * 2,
        [pltpu.VMEM((width, wide), BF), pltpu.SemaphoreType.DMA((DEVS,))],
        2 * rows * width * wide,
        24,
    )


def second_chunk(scalars, mine, other, groups, prev, width, ck, cot_col):
    counts, flat = flat_of(groups)
    rows = len(CREW) * TILE
    gx_spec = pl.BlockSpec((TILE, width // 2), lambda i, o: (i, 0))
    return kernel_call(
        lambda *a: second_kernel(*a, counts=counts),
        "second_chunk",
        scalars,
        [mine, other, mine] + flat + list(prev),
        [
            spec_of_cols(width, 0),
            spec_of_cols(width, 0),
            spec_of_cols(2 * ck, cot_col // (2 * ck)),
        ]
        + [pl.BlockSpec(memory_space=pltpu.HBM)] * len(flat)
        + [gx_spec] * 2,
        [gx_spec] * 2 + [pl.BlockSpec((TILE, ck), lambda i, o: (i, 0))],
        [jax.ShapeDtypeStruct((rows, width // 2), BF)] * 2
        + [jax.ShapeDtypeStruct((rows, ck), BF)],
        [
            pltpu.VMEM((width, 2 * ck), BF),
            pltpu.VMEM((TILE, width), BF),
            pltpu.SemaphoreType.DMA((DEVS,)),
        ],
        8 * rows * width * ck,
        24,
    )


def gate_grad(scalars, mine, other, d, width):
    rows, ck = d.shape
    steps = len(CREW)
    deep = width // steps
    x_spec = pl.BlockSpec((steps, TILE // 2, width // steps), lambda i, o: (0, 0, i))
    return kernel_call(
        gate_grad_kernel,
        "gate_grad",
        scalars,
        [mine, other, d],
        [x_spec, x_spec, pl.BlockSpec((rows, ck), lambda i, o: (0, 0))],
        [pl.BlockSpec((deep, ck), lambda i, o: (0, 0))] * len(CHAIN),
        [jax.ShapeDtypeStruct((deep, ck), BF)] * len(CHAIN),
        [pltpu.VMEM((rows, deep), BF), pltpu.VMEM((width, ck), BF)],
        2 * rows * width * ck,
        24,
    )


def join_kernel(scalars, *refs, quarter):
    out = refs[-1]
    for i, ref in enumerate(refs[:-1]):
        ck = ref.shape[1]
        start = scalars[DEVS + 2 + i % len(CREW)] * quarter
        if i >= len(CREW):
            start = start + refs[0].shape[1]
        out[:, pl.ds(pl.multiple_of(start, 128), ck)] = ref[...].astype(F32)


def join_call(scalars, pieces):
    depth = pieces[0].shape[0]
    quarter = pieces[0].shape[1] + pieces[-1].shape[1]
    vmem = pl.BlockSpec(memory_space=pltpu.VMEM)
    return pl.pallas_call(
        lambda *a: join_kernel(*a, quarter=quarter),
        in_specs=[pl.BlockSpec(memory_space=pltpu.SMEM)] + [vmem] * len(pieces),
        out_specs=vmem,
        out_shape=jax.ShapeDtypeStruct((depth, len(CREW) * quarter), F32),
        compiler_params=pltpu.CompilerParams(vmem_limit_bytes=16 * 1024 * 1024),
        name="join_quarters",
    )(scalars, *pieces)


def split_plan(x_in, cotangent, w_gate, w_up, send_counts, recv_counts):
    rows, width = x_in.shape
    depth, hidden = w_gate.shape
    crew = len(CREW)
    quarter = hidden // crew
    core = lax.axis_index("mp")
    index = lax.axis_index("dp")
    z, place = index // crew, index % crew
    places = [place ^ m for m in CREW]
    chunks = [640, 256]
    offsets = [0, chunks[0]]
    swap = [(0, 1), (1, 0)]

    def columns(array, q, offset, count):
        return lax.dynamic_slice_in_dim(array, q * quarter + offset, count, 1)

    def piece_of_weights(q, k):
        return jnp.concatenate(
            [columns(w, q, offsets[k], chunks[k]) for w in (w_gate, w_up)], axis=1
        )

    order = [z, z ^ 1, jnp.where(z < 2, 2, 1), jnp.where(z < 2, 3, 0)]
    inner = ((z == 1) | (z == 2)).astype(jnp.int32)
    scalars = [index ^ c ^ m for c in CHAIN for m in CREW] + [core, inner] + places
    scalars += [0] * (2 * DEVS - len(scalars)) + [p * crew + q for p in order for q in places]
    scalars = jnp.stack([jnp.asarray(v, jnp.int32) for v in scalars])

    first = [piece_of_weights(q, 0) for q in places]
    own = first[0]
    own_far = send(own, FAR)
    own_near = send(own, NEAR)
    rest = crew_swap(first)[1:]
    own_near, x_in, cotangent, w_gate, w_up = tie(own_near, x_in, cotangent, w_gate, w_up)
    parcels = pack_parcels(
        scalars, send_counts, recv_counts, x_in, cotangent, w_gate, w_up, chunks
    )
    rest = jnp.concatenate(rest, axis=0)
    rest, own_far, *parcels = tie(rest, own_far, *parcels)

    own_both = send(own_far, NEAR)
    rest_far = send(rest, FAR)
    rest_near = send(rest, NEAR)
    parcels = crew_swap(parcels)
    rest_far, rest_near, own_both, *parcels = tie(rest_far, rest_near, own_both, *parcels)

    rest_both = send(rest_far, NEAR)
    mine = jnp.stack(parcels)
    other = lax.ppermute(mine, "mp", swap)
    second = mine[:, :, width + 2 * quarter :].reshape(crew * depth, 2 * chunks[1])
    rest_both, other, second = tie(rest_both, other, second)

    cot_second = width
    cot_first = width + 2 * chunks[1]

    second_near = send(second, NEAR)
    second_far = send(second, FAR)
    groups = [(own, own_near, own_far, own_both), (rest, rest_near, rest_far, rest_both)]
    d_first, parts = first_chunk(scalars, mine, other, groups, width, chunks[0], cot_first)
    second_near, second_far, d_first = tie(second_near, second_far, d_first)
    p0, p1, p2, p3 = parts

    middle = along(second, INNER)
    ends = along(second_far, TO_ENDS)
    r1 = along(p3, FROM_ENDS)
    gx = rows_grad(scalars, d_first, groups, width)
    r1, middle, ends, p2, p3, *gx = tie(r1, middle, ends, p2, p3, *gx)
    r2b = along(p2, FROM_ENDS)
    r2a = along(add(p3, r1), INNER)
    keep, give, d_second = second_chunk(
        scalars, mine, other, [(second, second_near, second_far, middle, ends)], gx,
        width, chunks[1], cot_second,
    )
    r2a, r2b, keep, give, d_second = tie(r2a, r2b, keep, give, d_second)

    theirs = lax.ppermute(give, "mp", swap)
    q_parts = gate_grad(scalars, mine, other, d_second, width)
    theirs, *q_parts = tie(theirs, *q_parts)
    q_own, q_near, q_far, q_both = q_parts
    from_near = send(q_both, NEAR)
    r3b = along(add(p2, r2b), INNER)
    r3a = along(add(p1, r2a), OUTER)
    rows_x = crew_swap(
        [
            add(keep[s * rows : (s + 1) * rows], theirs[s * rows : (s + 1) * rows])
            for s in range(crew)
        ]
    )
    from_near, r3a, r3b = tie(from_near, r3a, r3b)
    sum_far = send(add(q_far, from_near), FAR)
    sum_near = send(q_near, NEAR)
    sums = add(p0, r3a, r3b)
    firsts = crew_swap([sums[s * depth : (s + 1) * depth] for s in range(crew)])
    sum_far, sum_near, *rows_x = tie(sum_far, sum_near, *rows_x)
    sums = add(q_own, sum_near, sum_far)
    lasts = crew_swap([sums[s * depth : (s + 1) * depth] for s in range(crew)])
    return add(*rows_x), join_call(scalars, firsts + lasts)


def solution(mesh):
    sizes = dict(mesh.shape)
    splits = sizes["dp"] == DEVS and sizes["mp"] == 2
    return jax.shard_map(
        split_plan if splits else general_plan,
        mesh=mesh,
        in_specs=(
            P("dp", None),
            P("dp", "mp"),
            P("dp", "mp"),
            P("dp", "mp"),
            P("dp", None),
            P("dp", None),
        ),
        out_specs=(P("dp", "mp"), P("dp", "mp")),
        check_vma=False,
    )
```

```python
import jax
import jax.numpy as jnp
from jax import lax
from jax.experimental import pallas as pl
from jax.experimental.pallas import tpu as pltpu
from jax.sharding import PartitionSpec as P

BAL = 208
BF = jnp.bfloat16
F32 = jnp.float32


def contract_last(left, right):
    return lax.dot_general(
        left, right, (((1,), (1,)), ((), ())), preferred_element_type=F32
    )


def contract_first(left, right):
    return lax.dot_general(
        left, right, (((0,), (0,)), ((), ())), preferred_element_type=F32
    )


def swiglu_back(x_rows, cot_rows, gate_full, up_full, live_mask):
    gate_val = jnp.dot(x_rows, gate_full, preferred_element_type=F32)
    up_val = jnp.dot(x_rows, up_full, preferred_element_type=F32)
    sig = jax.nn.sigmoid(gate_val)
    cot_val = cot_rows.astype(F32)
    d_gate = jnp.where(
        live_mask[:, None], cot_val * up_val * sig * (1.0 + gate_val * (1.0 - sig)), 0.0
    ).astype(BF)
    d_up = jnp.where(live_mask[:, None], cot_val * gate_val * sig, 0.0).astype(BF)
    return contract_last(d_gate, gate_full) + contract_last(d_up, up_full), d_gate


def live_rows_of(send_counts, recv_counts):
    return BAL + jnp.sum(send_counts[0]) - jnp.sum(recv_counts[0])


def general_plan(x_in, cotangent, w_gate, w_up, send_counts, recv_counts):
    dev_count = lax.axis_size("dp")
    gate_full = lax.all_gather(w_gate, "dp", axis=0, tiled=True)
    up_full = lax.all_gather(w_up, "dp", axis=0, tiled=True)
    live_mask = jnp.arange(x_in.shape[0]) < live_rows_of(send_counts, recv_counts)
    partial_value, d_gate = swiglu_back(x_in, cotangent, gate_full, up_full, live_mask)
    grad_x = lax.psum_scatter(
        partial_value.astype(BF), "mp", scatter_dimension=1, tiled=True
    )
    whole = contract_first(x_in, d_gate)
    pieces = lax.all_to_all(
        whole.reshape(dev_count, x_in.shape[1] // dev_count, whole.shape[1]),
        "dp",
        split_axis=0,
        concat_axis=0,
        tiled=True,
    )
    return grad_x, jnp.sum(pieces, axis=0)


CREW = (0, 1, 2, 3)
NEAR, FAR = 4, 8
CHAIN = (0, NEAR, FAR, NEAR | FAR)
DEVS = 16
TILE = 256


def tie(*values):
    return lax.optimization_barrier(values)


def send(value, mask):
    return lax.ppermute(value, "dp", [(i, i ^ mask) for i in range(DEVS)])


def along(value, moves):
    crew = len(CREW)
    return lax.ppermute(
        value, "dp", [(crew * a + q, crew * b + q) for a, b in moves for q in range(crew)]
    )


OUTER = [(0, 1), (1, 0), (2, 3), (3, 2)]
INNER = [(1, 2), (2, 1)]
TO_ENDS = [(1, 0), (2, 3)]
FROM_ENDS = [(0, 1), (3, 2)]


def crew_swap(pieces):
    return [send(p, m) if m else p for p, m in zip(pieces, CREW)]


def add(*terms):
    total = terms[0].astype(F32)
    for term in terms[1:]:
        total = total + term.astype(F32)
    return total.astype(BF)


def place_weights(scalars, groups, w_all, sems, act):
    blk = w_all.shape[0] // DEVS
    crew = len(CREW)
    inner = scalars[DEVS + 1]
    base = 0
    for n, members in groups:
        for c, member in enumerate(members):
            for i in range(n // blk):
                j = min(c, len(CHAIN) - 1) * crew + base + i
                start = pl.multiple_of(scalars[j] * blk, blk)
                copy = pltpu.make_async_copy(
                    member.at[pl.ds(i * blk, blk), :], w_all.at[pl.ds(start, blk), :], sems.at[j]
                )
                if len(members) > len(CHAIN) and c >= len(CHAIN) - 1:
                    pl.when(inner == (1 if c == len(CHAIN) - 1 else 0))(
                        lambda copy=copy: act(copy)
                    )
                else:
                    act(copy)
        base += n // blk


def grouped(refs, counts):
    groups = []
    for n, members in counts:
        groups.append((n, refs[:members]))
        refs = refs[members:]
    return groups, refs


def place_rows(core, tile, mine_ref, other_ref, cols=slice(None)):
    rows = TILE // 2
    lower = pl.ds(pl.multiple_of(core * rows, rows), rows)
    upper = pl.ds(pl.multiple_of((1 - core) * rows, rows), rows)
    tile[lower, :] = mine_ref[0, :, cols]
    tile[upper, :] = other_ref[0, :, cols]


def store_rows_grad(core, gx, gx_refs, prev):
    half = gx.shape[1] // 2
    low, high = gx[:, :half], gx[:, half:]
    for keep in range(2):

        @pl.when(core == keep)
        def _():
            for i, value in enumerate(((low, high)[keep], (high, low)[keep])):
                if prev is not None:
                    value = value + prev[i][...].astype(F32)
                gx_refs[i][...] = value.astype(BF)


def front(x, w_all, cot_lower, cot_upper):
    ck = w_all.shape[1] // 2
    both = jnp.dot(x, w_all[...], preferred_element_type=F32)
    gate, up = both[:, :ck], both[:, ck:]
    cot = jnp.concatenate([cot_lower, cot_upper], axis=0).astype(F32)
    sig = jax.nn.sigmoid(gate)
    d_gate = (cot * up * sig * (1.0 + gate * (1.0 - sig))).astype(BF)
    d_up = (cot * gate * sig).astype(BF)
    return d_gate, d_up


def pack_kernel(scalars, sent, got, x_ref, cot_ref, gate_ref, up_ref, *outs, chunks, quarter):
    rows, width = x_ref.shape
    half = rows // 2
    live = BAL
    for i in range(sent.shape[1]):
        live = live + sent[0, i] - got[0, i]
    is_live = lax.broadcasted_iota(jnp.int32, (rows, 1), 0) < live
    x_half = x_ref[pl.ds(pl.multiple_of(scalars[DEVS] * half, half), half), :]
    for s, out in enumerate(outs):
        start = scalars[DEVS + 2 + s] * quarter
        out[:, :width] = x_half
        col = width
        for k in (1, 0):
            spot = pl.ds(pl.multiple_of(start + sum(chunks[:k]), 128), chunks[k])
            cot = jnp.where(is_live, cot_ref[:, spot].astype(F32), 0.0).astype(BF)
            for part in (cot[:half], cot[half:]):
                out[:, col : col + chunks[k]] = part
                col += chunks[k]
        spot = pl.ds(pl.multiple_of(start + chunks[0], 128), chunks[1])
        for ref in (gate_ref, up_ref):
            out[:, col : col + chunks[1]] = ref[:, spot]
            col += chunks[1]


def pack_parcels(scalars, sent, got, x_in, cotangent, w_gate, w_up, chunks):
    rows, width = x_in.shape
    quarter = sum(chunks)
    vmem = pl.BlockSpec(memory_space=pltpu.VMEM)
    smem = pl.BlockSpec(memory_space=pltpu.SMEM)
    wide = width + 2 * quarter + 2 * chunks[1]
    return pl.pallas_call(
        lambda *a: pack_kernel(*a, chunks=chunks, quarter=quarter),
        in_specs=[smem] * 3 + [vmem] * 4,
        out_specs=[vmem] * len(CREW),
        out_shape=[jax.ShapeDtypeStruct((rows // 2, wide), BF)] * len(CREW),
        compiler_params=pltpu.CompilerParams(vmem_limit_bytes=32 * 1024 * 1024),
        cost_estimate=pl.CostEstimate(flops=0, bytes_accessed=2**23, transcendentals=0),
        name="pack_parcels",
    )(scalars, sent, got, x_in, cotangent, w_gate, w_up)


def pieces_kernel(scalars, gate_ref, up_ref, *outs, ck, quarter):
    for s, out in enumerate(outs):
        start = scalars[DEVS + 2 + s] * quarter
        spot = pl.ds(pl.multiple_of(start, 128), ck)
        out[:, :ck] = gate_ref[:, spot]
        out[:, ck:] = up_ref[:, spot]


def pieces_of_first(scalars, w_gate, w_up, ck, quarter):
    vmem = pl.BlockSpec(memory_space=pltpu.VMEM)
    return pl.pallas_call(
        lambda *a: pieces_kernel(*a, ck=ck, quarter=quarter),
        in_specs=[pl.BlockSpec(memory_space=pltpu.SMEM), vmem, vmem],
        out_specs=[vmem] * len(CREW),
        out_shape=[jax.ShapeDtypeStruct((w_gate.shape[0], 2 * ck), BF)] * len(CREW),
        compiler_params=pltpu.CompilerParams(vmem_limit_bytes=16 * 1024 * 1024),
        cost_estimate=pl.CostEstimate(flops=0, bytes_accessed=2**22, transcendentals=0),
        name="pieces_of_first",
    )(scalars, w_gate, w_up)


def first_kernel(scalars, mine_ref, other_ref, low_ref, high_ref, *refs, counts):
    groups, refs = grouped(refs, counts)
    d_ref, refs = refs[0], refs[1:]
    gg_refs, (w_all, x_all, d_all, acc, sems) = refs[: len(CHAIN)], refs[len(CHAIN) :]
    step = pl.program_id(0)
    width = w_all.shape[0]
    blk = width // DEVS
    crew = len(CREW)

    @pl.when(step == 0)
    def _():
        place_weights(scalars, groups, w_all, sems, lambda copy: copy.start())

    here = pl.ds(pl.multiple_of(step * TILE, TILE), TILE)
    place_rows(scalars[DEVS], x_all.at[here], mine_ref, other_ref)

    @pl.when(step == 0)
    def _():
        place_weights(scalars, groups, w_all, sems, lambda copy: copy.wait())

    d_gate, d_up = front(x_all[here, :], w_all, low_ref[0], high_ref[0])
    d_all[here, :] = d_gate
    d_ref[...] = jnp.concatenate([d_gate, d_up], axis=1)

    @pl.when(step == pl.num_programs(0) - 1)
    def _():
        d = d_all[...]
        deep = crew * blk
        for r in range(len(CHAIN)):
            cols = slice(r * deep, (r + 1) * deep)
            acc[cols, :] = contract_first(x_all[:, cols], d).astype(BF)
        for j in range(DEVS):
            row = (j % crew) * blk
            at_row = pl.multiple_of(scalars[2 * DEVS + j] * blk, blk)
            gg_refs[j // crew][row : row + blk, :] = acc[pl.ds(at_row, blk), :]


def rows_grad_kernel(scalars, d_ref, *refs, counts):
    groups, refs = grouped(refs, counts)
    gx_refs, (w_all, sems) = refs[:2], refs[2:]

    @pl.when(pl.program_id(0) == 0)
    def _():
        place_weights(scalars, groups, w_all, sems, lambda copy: copy.start())
        place_weights(scalars, groups, w_all, sems, lambda copy: copy.wait())

    store_rows_grad(scalars[DEVS], contract_last(d_ref[...], w_all[...]), gx_refs, None)


def second_kernel(scalars, mine_ref, other_ref, cot_ref, *refs, counts):
    groups, refs = grouped(refs, counts)
    prev, gx_refs, (d_ref, w_all, x_tile, sems) = refs[:2], refs[2:4], refs[4:]
    step = pl.program_id(0)
    ck = d_ref.shape[1]

    @pl.when(step == 0)
    def _():
        place_weights(scalars, groups, w_all, sems, lambda copy: copy.start())

    place_rows(scalars[DEVS], x_tile, mine_ref, other_ref)

    @pl.when(step == 0)
    def _():
        place_weights(scalars, groups, w_all, sems, lambda copy: copy.wait())

    d_gate, d_up = front(x_tile[...], w_all, cot_ref[0, :, :ck], cot_ref[0, :, ck:])
    d_ref[...] = d_gate
    gx = contract_last(jnp.concatenate([d_gate, d_up], axis=1), w_all[...])
    store_rows_grad(scalars[DEVS], gx, gx_refs, prev)


def gate_grad_kernel(scalars, mine_ref, other_ref, d_ref, *refs):
    out_refs, (x_all, acc) = refs[: len(CHAIN)], refs[len(CHAIN) :]
    step = pl.program_id(0)
    core = scalars[DEVS]
    crew = len(CREW)
    for s in range(crew):
        tile = x_all.at[s * TILE : (s + 1) * TILE]
        place_rows(core, tile, mine_ref.at[s : s + 1], other_ref.at[s : s + 1])
    deep = x_all.shape[1]
    here = pl.ds(pl.multiple_of(step * deep, deep), deep)
    acc[here, :] = contract_first(x_all[...], d_ref[...]).astype(BF)

    @pl.when(step == pl.num_programs(0) - 1)
    def _():
        blk = deep // crew
        for j in range(DEVS):
            row = (j % crew) * blk
            at_row = pl.multiple_of(scalars[j] * blk, blk)
            out_refs[j // crew][row : row + blk, :] = acc[pl.ds(at_row, blk), :]


def kernel_call(body, name, scalars, operands, in_specs, out_specs, out_shape, scratch, flops, limit):
    return pl.pallas_call(
        body,
        grid_spec=pltpu.PrefetchScalarGridSpec(
            num_scalar_prefetch=1,
            grid=(len(CREW),),
            in_specs=in_specs,
            out_specs=out_specs,
            scratch_shapes=scratch,
        ),
        out_shape=out_shape,
        compiler_params=pltpu.CompilerParams(vmem_limit_bytes=limit * 1024 * 1024),
        cost_estimate=pl.CostEstimate(flops=flops, bytes_accessed=2**23, transcendentals=0),
        name=name,
    )(scalars, *operands)


def spec_of_cols(wide, col):
    return pl.BlockSpec((1, TILE // 2, wide), lambda i, o: (i, 0, col))


def flat_of(groups):
    counts = [(g[0].shape[0], len(g)) for g in groups]
    return counts, [v for g in groups for v in g]


def first_chunk(scalars, mine, other, groups, width, ck, cot_col):
    counts, flat = flat_of(groups)
    rows = len(CREW) * TILE
    deep = width // len(CHAIN)
    d, *parts = kernel_call(
        lambda *a: first_kernel(*a, counts=counts),
        "first_chunk",
        scalars,
        [mine, other, mine, mine] + flat,
        [
            spec_of_cols(width, 0),
            spec_of_cols(width, 0),
            spec_of_cols(ck, cot_col // ck),
            spec_of_cols(ck, cot_col // ck + 1),
        ]
        + [pl.BlockSpec(memory_space=pltpu.HBM)] * len(flat),
        [pl.BlockSpec((TILE, 2 * ck), lambda i, o: (i, 0))]
        + [pl.BlockSpec((deep, ck), lambda i, o: (0, 0))] * len(CHAIN),
        [jax.ShapeDtypeStruct((rows, 2 * ck), BF)]
        + [jax.ShapeDtypeStruct((deep, ck), BF)] * len(CHAIN),
        [
            pltpu.VMEM((width, 2 * ck), BF),
            pltpu.VMEM((rows, width), BF),
            pltpu.VMEM((rows, ck), BF),
            pltpu.VMEM((width, ck), BF),
            pltpu.SemaphoreType.DMA((DEVS,)),
        ],
        6 * rows * width * ck,
        32,
    )
    return d, parts


def rows_grad(scalars, d, groups, width):
    counts, flat = flat_of(groups)
    rows, wide = d.shape
    gx_spec = pl.BlockSpec((TILE, width // 2), lambda i, o: (i, 0))
    return kernel_call(
        lambda *a: rows_grad_kernel(*a, counts=counts),
        "rows_grad",
        scalars,
        [d] + flat,
        [pl.BlockSpec((TILE, wide), lambda i, o: (i, 0))]
        + [pl.BlockSpec(memory_space=pltpu.HBM)] * len(flat),
        [gx_spec] * 2,
        [jax.ShapeDtypeStruct((rows, width // 2), BF)] * 2,
        [pltpu.VMEM((width, wide), BF), pltpu.SemaphoreType.DMA((DEVS,))],
        2 * rows * width * wide,
        24,
    )


def second_chunk(scalars, mine, other, groups, prev, width, ck, cot_col):
    counts, flat = flat_of(groups)
    rows = len(CREW) * TILE
    gx_spec = pl.BlockSpec((TILE, width // 2), lambda i, o: (i, 0))
    return kernel_call(
        lambda *a: second_kernel(*a, counts=counts),
        "second_chunk",
        scalars,
        [mine, other, mine] + flat + list(prev),
        [
            spec_of_cols(width, 0),
            spec_of_cols(width, 0),
            spec_of_cols(2 * ck, cot_col // (2 * ck)),
        ]
        + [pl.BlockSpec(memory_space=pltpu.HBM)] * len(flat)
        + [gx_spec] * 2,
        [gx_spec] * 2 + [pl.BlockSpec((TILE, ck), lambda i, o: (i, 0))],
        [jax.ShapeDtypeStruct((rows, width // 2), BF)] * 2
        + [jax.ShapeDtypeStruct((rows, ck), BF)],
        [
            pltpu.VMEM((width, 2 * ck), BF),
            pltpu.VMEM((TILE, width), BF),
            pltpu.SemaphoreType.DMA((DEVS,)),
        ],
        8 * rows * width * ck,
        24,
    )


def gate_grad(scalars, mine, other, d, width):
    rows, ck = d.shape
    steps = len(CREW)
    deep = width // steps
    x_spec = pl.BlockSpec((steps, TILE // 2, width // steps), lambda i, o: (0, 0, i))
    return kernel_call(
        gate_grad_kernel,
        "gate_grad",
        scalars,
        [mine, other, d],
        [x_spec, x_spec, pl.BlockSpec((rows, ck), lambda i, o: (0, 0))],
        [pl.BlockSpec((deep, ck), lambda i, o: (0, 0))] * len(CHAIN),
        [jax.ShapeDtypeStruct((deep, ck), BF)] * len(CHAIN),
        [pltpu.VMEM((rows, deep), BF), pltpu.VMEM((width, ck), BF)],
        2 * rows * width * ck,
        24,
    )


def join_kernel(scalars, *refs, quarter):
    out = refs[-1]
    for i, ref in enumerate(refs[:-1]):
        ck = ref.shape[1]
        start = scalars[DEVS + 2 + i % len(CREW)] * quarter
        if i >= len(CREW):
            start = start + refs[0].shape[1]
        out[:, pl.ds(pl.multiple_of(start, 128), ck)] = ref[...].astype(F32)


def join_call(scalars, pieces):
    depth = pieces[0].shape[0]
    quarter = pieces[0].shape[1] + pieces[-1].shape[1]
    vmem = pl.BlockSpec(memory_space=pltpu.VMEM)
    return pl.pallas_call(
        lambda *a: join_kernel(*a, quarter=quarter),
        in_specs=[pl.BlockSpec(memory_space=pltpu.SMEM)] + [vmem] * len(pieces),
        out_specs=vmem,
        out_shape=jax.ShapeDtypeStruct((depth, len(CREW) * quarter), F32),
        compiler_params=pltpu.CompilerParams(vmem_limit_bytes=16 * 1024 * 1024),
        name="join_quarters",
    )(scalars, *pieces)


def split_plan(x_in, cotangent, w_gate, w_up, send_counts, recv_counts):
    rows, width = x_in.shape
    depth, hidden = w_gate.shape
    crew = len(CREW)
    quarter = hidden // crew
    core = lax.axis_index("mp")
    index = lax.axis_index("dp")
    z, place = index // crew, index % crew
    places = [place ^ m for m in CREW]
    chunks = [640, 256]
    swap = [(0, 1), (1, 0)]

    order = [z, z ^ 1, jnp.where(z < 2, 2, 1), jnp.where(z < 2, 3, 0)]
    inner = ((z == 1) | (z == 2)).astype(jnp.int32)
    scalars = [index ^ c ^ m for c in CHAIN for m in CREW] + [core, inner] + places
    scalars += [0] * (2 * DEVS - len(scalars)) + [p * crew + q for p in order for q in places]
    scalars = jnp.stack([jnp.asarray(v, jnp.int32) for v in scalars])

    first = pieces_of_first(scalars, w_gate, w_up, chunks[0], quarter)
    own = first[0]
    own_far = send(own, FAR)
    own_near = send(own, NEAR)
    rest = crew_swap(first)[1:]
    own_near, x_in, cotangent, w_gate, w_up = tie(own_near, x_in, cotangent, w_gate, w_up)
    parcels = pack_parcels(
        scalars, send_counts, recv_counts, x_in, cotangent, w_gate, w_up, chunks
    )
    rest = jnp.concatenate(rest, axis=0)
    rest, own_far, *parcels = tie(rest, own_far, *parcels)

    own_both = send(own_far, NEAR)
    rest_far = send(rest, FAR)
    rest_near = send(rest, NEAR)
    parcels = crew_swap(parcels)
    rest_far, rest_near, own_both, *parcels = tie(rest_far, rest_near, own_both, *parcels)

    rest_both = send(rest_far, NEAR)
    mine = jnp.stack(parcels)
    other = lax.ppermute(mine, "mp", swap)
    second = mine[:, :, width + 2 * quarter :].reshape(crew * depth, 2 * chunks[1])
    rest_both, other, second = tie(rest_both, other, second)

    cot_second = width
    cot_first = width + 2 * chunks[1]

    second_near = send(second, NEAR)
    second_far = send(second, FAR)
    groups = [(own, own_near, own_far, own_both), (rest, rest_near, rest_far, rest_both)]
    d_first, parts = first_chunk(scalars, mine, other, groups, width, chunks[0], cot_first)
    second_near, second_far, d_first = tie(second_near, second_far, d_first)
    p0, p1, p2, p3 = parts

    middle = along(second, INNER)
    ends = along(second_far, TO_ENDS)
    r1 = along(p3, FROM_ENDS)
    gx = rows_grad(scalars, d_first, groups, width)
    r1, middle, ends, p2, p3, *gx = tie(r1, middle, ends, p2, p3, *gx)
    r2b = along(p2, FROM_ENDS)
    r2a = along(add(p3, r1), INNER)
    keep, give, d_second = second_chunk(
        scalars, mine, other, [(second, second_near, second_far, middle, ends)], gx,
        width, chunks[1], cot_second,
    )
    r2a, r2b, keep, give, d_second = tie(r2a, r2b, keep, give, d_second)

    theirs = lax.ppermute(give, "mp", swap)
    q_parts = gate_grad(scalars, mine, other, d_second, width)
    theirs, *q_parts = tie(theirs, *q_parts)
    q_own, q_near, q_far, q_both = q_parts
    from_near = send(q_both, NEAR)
    r3b = along(add(p2, r2b), INNER)
    r3a = along(add(p1, r2a), OUTER)
    rows_x = crew_swap(
        [
            add(keep[s * rows : (s + 1) * rows], theirs[s * rows : (s + 1) * rows])
            for s in range(crew)
        ]
    )
    from_near, r3a, r3b = tie(from_near, r3a, r3b)
    sum_far = send(add(q_far, from_near), FAR)
    sum_near = send(q_near, NEAR)
    sums = add(p0, r3a, r3b)
    firsts = crew_swap([sums[s * depth : (s + 1) * depth] for s in range(crew)])
    sum_far, sum_near, *rows_x = tie(sum_far, sum_near, *rows_x)
    sums = add(q_own, sum_near, sum_far)
    lasts = crew_swap([sums[s * depth : (s + 1) * depth] for s in range(crew)])
    return add(*rows_x), join_call(scalars, firsts + lasts)


def solution(mesh):
    sizes = dict(mesh.shape)
    splits = sizes["dp"] == DEVS and sizes["mp"] == 2
    return jax.shard_map(
        split_plan if splits else general_plan,
        mesh=mesh,
        in_specs=(
            P("dp", None),
            P("dp", "mp"),
            P("dp", "mp"),
            P("dp", "mp"),
            P("dp", None),
            P("dp", None),
        ),
        out_specs=(P("dp", "mp"), P("dp", "mp")),
        check_vma=False,
    )
```

```python
import jax
import jax.numpy as jnp
from jax import lax
from jax.experimental import pallas as pl
from jax.experimental.pallas import tpu as pltpu
from jax.sharding import PartitionSpec as P

BAL = 208
BF = jnp.bfloat16
F32 = jnp.float32


def contract_last(left, right):
    return lax.dot_general(
        left, right, (((1,), (1,)), ((), ())), preferred_element_type=F32
    )


def contract_first(left, right):
    return lax.dot_general(
        left, right, (((0,), (0,)), ((), ())), preferred_element_type=F32
    )


def swiglu_back(x_rows, cot_rows, gate_full, up_full, live_mask):
    gate_val = jnp.dot(x_rows, gate_full, preferred_element_type=F32)
    up_val = jnp.dot(x_rows, up_full, preferred_element_type=F32)
    sig = jax.nn.sigmoid(gate_val)
    cot_val = cot_rows.astype(F32)
    d_gate = jnp.where(
        live_mask[:, None], cot_val * up_val * sig * (1.0 + gate_val * (1.0 - sig)), 0.0
    ).astype(BF)
    d_up = jnp.where(live_mask[:, None], cot_val * gate_val * sig, 0.0).astype(BF)
    return contract_last(d_gate, gate_full) + contract_last(d_up, up_full), d_gate


def live_rows_of(send_counts, recv_counts):
    return BAL + jnp.sum(send_counts[0]) - jnp.sum(recv_counts[0])


def general_plan(x_in, cotangent, w_gate, w_up, send_counts, recv_counts):
    dev_count = lax.axis_size("dp")
    gate_full = lax.all_gather(w_gate, "dp", axis=0, tiled=True)
    up_full = lax.all_gather(w_up, "dp", axis=0, tiled=True)
    live_mask = jnp.arange(x_in.shape[0]) < live_rows_of(send_counts, recv_counts)
    partial_value, d_gate = swiglu_back(x_in, cotangent, gate_full, up_full, live_mask)
    grad_x = lax.psum_scatter(
        partial_value.astype(BF), "mp", scatter_dimension=1, tiled=True
    )
    whole = contract_first(x_in, d_gate)
    pieces = lax.all_to_all(
        whole.reshape(dev_count, x_in.shape[1] // dev_count, whole.shape[1]),
        "dp",
        split_axis=0,
        concat_axis=0,
        tiled=True,
    )
    return grad_x, jnp.sum(pieces, axis=0)


CREW = (0, 1, 2, 3)
NEAR, FAR = 4, 8
CHAIN = (0, NEAR, FAR, NEAR | FAR)
DEVS = 16
TILE = 256


def tie(*values):
    return lax.optimization_barrier(values)


def send(value, mask):
    return lax.ppermute(value, "dp", [(i, i ^ mask) for i in range(DEVS)])


def along(value, moves):
    crew = len(CREW)
    return lax.ppermute(
        value, "dp", [(crew * a + q, crew * b + q) for a, b in moves for q in range(crew)]
    )


OUTER = [(0, 1), (1, 0), (2, 3), (3, 2)]
INNER = [(1, 2), (2, 1)]
TO_ENDS = [(1, 0), (2, 3)]
FROM_ENDS = [(0, 1), (3, 2)]


def crew_swap(pieces):
    return [send(p, m) if m else p for p, m in zip(pieces, CREW)]


def add(*terms):
    total = terms[0].astype(F32)
    for term in terms[1:]:
        total = total + term.astype(F32)
    return total.astype(BF)


def place_weights(scalars, groups, w_all, sems, act):
    blk = w_all.shape[0] // DEVS
    crew = len(CREW)
    inner = scalars[DEVS + 1]
    base = 0
    for n, members in groups:
        for c, member in enumerate(members):
            for i in range(n // blk):
                j = min(c, len(CHAIN) - 1) * crew + base + i
                start = pl.multiple_of(scalars[j] * blk, blk)
                copy = pltpu.make_async_copy(
                    member.at[pl.ds(i * blk, blk), :], w_all.at[pl.ds(start, blk), :], sems.at[j]
                )
                if len(members) > len(CHAIN) and c >= len(CHAIN) - 1:
                    pl.when(inner == (1 if c == len(CHAIN) - 1 else 0))(
                        lambda copy=copy: act(copy)
                    )
                else:
                    act(copy)
        base += n // blk


def grouped(refs, counts):
    groups = []
    for n, members in counts:
        groups.append((n, refs[:members]))
        refs = refs[members:]
    return groups, refs


def place_rows(core, tile, mine_ref, other_ref, cols=slice(None)):
    rows = TILE // 2
    lower = pl.ds(pl.multiple_of(core * rows, rows), rows)
    upper = pl.ds(pl.multiple_of((1 - core) * rows, rows), rows)
    tile[lower, :] = mine_ref[0, :, cols]
    tile[upper, :] = other_ref[0, :, cols]


def store_rows_grad(core, gx, gx_refs, prev):
    half = gx.shape[1] // 2
    low, high = gx[:, :half], gx[:, half:]
    for keep in range(2):

        @pl.when(core == keep)
        def _():
            for i, value in enumerate(((low, high)[keep], (high, low)[keep])):
                if prev is not None:
                    value = value + prev[i][...].astype(F32)
                gx_refs[i][...] = value.astype(BF)


def front(x, w_all, cot_lower, cot_upper):
    ck = w_all.shape[1] // 2
    both = jnp.dot(x, w_all[...], preferred_element_type=F32)
    gate, up = both[:, :ck], both[:, ck:]
    cot = jnp.concatenate([cot_lower, cot_upper], axis=0).astype(F32)
    sig = jax.nn.sigmoid(gate)
    d_gate = (cot * up * sig * (1.0 + gate * (1.0 - sig))).astype(BF)
    d_up = (cot * gate * sig).astype(BF)
    return d_gate, d_up


def pack_kernel(scalars, sent, got, x_ref, cot_ref, gate_ref, up_ref, *refs, chunks, quarter):
    outs, sems = refs[: len(CREW)], refs[len(CREW)]
    rows, width = x_ref.shape
    half = rows // 2
    copies = []
    for s, out in enumerate(outs):
        start = scalars[DEVS + 2 + s] * quarter + chunks[0]
        spot = pl.ds(pl.multiple_of(start, 128), chunks[1])
        for i, ref in enumerate((gate_ref, up_ref)):
            col = width + 2 * quarter + i * chunks[1]
            there = out.at[:, col : col + chunks[1]]
            copies.append(pltpu.make_async_copy(ref.at[:, spot], there, sems.at[2 * s + i]))
    for copy in copies:
        copy.start()
    live = BAL
    for i in range(sent.shape[1]):
        live = live + sent[0, i] - got[0, i]
    is_live = lax.broadcasted_iota(jnp.int32, (rows, 1), 0) < live
    x_half = x_ref[pl.ds(pl.multiple_of(scalars[DEVS] * half, half), half), :]
    for s, out in enumerate(outs):
        start = scalars[DEVS + 2 + s] * quarter
        out[:, :width] = x_half
        col = width
        for k in (1, 0):
            spot = pl.ds(pl.multiple_of(start + sum(chunks[:k]), 128), chunks[k])
            cot = jnp.where(is_live, cot_ref[:, spot].astype(F32), 0.0).astype(BF)
            for part in (cot[:half], cot[half:]):
                out[:, col : col + chunks[k]] = part
                col += chunks[k]
    for copy in copies:
        copy.wait()


def pack_parcels(scalars, sent, got, x_in, cotangent, w_gate, w_up, chunks):
    rows, width = x_in.shape
    quarter = sum(chunks)
    vmem = pl.BlockSpec(memory_space=pltpu.VMEM)
    smem = pl.BlockSpec(memory_space=pltpu.SMEM)
    wide = width + 2 * quarter + 2 * chunks[1]
    return pl.pallas_call(
        lambda *a: pack_kernel(*a, chunks=chunks, quarter=quarter),
        in_specs=[smem] * 3 + [vmem] * 2 + [pl.BlockSpec(memory_space=pltpu.HBM)] * 2,
        out_specs=[vmem] * len(CREW),
        scratch_shapes=[pltpu.SemaphoreType.DMA((2 * len(CREW),))],
        out_shape=[jax.ShapeDtypeStruct((rows // 2, wide), BF)] * len(CREW),
        compiler_params=pltpu.CompilerParams(vmem_limit_bytes=32 * 1024 * 1024),
        cost_estimate=pl.CostEstimate(flops=0, bytes_accessed=2**23, transcendentals=0),
        name="pack_parcels",
    )(scalars, sent, got, x_in, cotangent, w_gate, w_up)


def pieces_kernel(scalars, gate_ref, up_ref, *refs, ck, quarter):
    outs, sems = refs[: len(CREW)], refs[len(CREW)]
    copies = []
    for s, out in enumerate(outs):
        start = scalars[DEVS + 2 + s] * quarter
        spot = pl.ds(pl.multiple_of(start, 128), ck)
        for i, ref in enumerate((gate_ref, up_ref)):
            there = out.at[:, i * ck : (i + 1) * ck]
            copies.append(pltpu.make_async_copy(ref.at[:, spot], there, sems.at[2 * s + i]))
    for copy in copies:
        copy.start()
    for copy in copies:
        copy.wait()


def pieces_of_first(scalars, w_gate, w_up, ck, quarter):
    vmem = pl.BlockSpec(memory_space=pltpu.VMEM)
    return pl.pallas_call(
        lambda *a: pieces_kernel(*a, ck=ck, quarter=quarter),
        in_specs=[pl.BlockSpec(memory_space=pltpu.SMEM)]
        + [pl.BlockSpec(memory_space=pltpu.HBM)] * 2,
        out_specs=[vmem] * len(CREW),
        scratch_shapes=[pltpu.SemaphoreType.DMA((2 * len(CREW),))],
        out_shape=[jax.ShapeDtypeStruct((w_gate.shape[0], 2 * ck), BF)] * len(CREW),
        compiler_params=pltpu.CompilerParams(vmem_limit_bytes=16 * 1024 * 1024),
        cost_estimate=pl.CostEstimate(flops=0, bytes_accessed=2**22, transcendentals=0),
        name="pieces_of_first",
    )(scalars, w_gate, w_up)


def first_kernel(scalars, mine_ref, other_ref, low_ref, high_ref, *refs, counts):
    groups, refs = grouped(refs, counts)
    d_ref, refs = refs[0], refs[1:]
    gg_refs, (w_all, x_all, d_all, acc, sems) = refs[: len(CHAIN)], refs[len(CHAIN) :]
    step = pl.program_id(0)
    width = w_all.shape[0]
    blk = width // DEVS
    crew = len(CREW)

    @pl.when(step == 0)
    def _():
        place_weights(scalars, groups, w_all, sems, lambda copy: copy.start())

    here = pl.ds(pl.multiple_of(step * TILE, TILE), TILE)
    place_rows(scalars[DEVS], x_all.at[here], mine_ref, other_ref)

    @pl.when(step == 0)
    def _():
        place_weights(scalars, groups, w_all, sems, lambda copy: copy.wait())

    d_gate, d_up = front(x_all[here, :], w_all, low_ref[0], high_ref[0])
    d_all[here, :] = d_gate
    d_ref[...] = jnp.concatenate([d_gate, d_up], axis=1)

    @pl.when(step == pl.num_programs(0) - 1)
    def _():
        d = d_all[...]
        deep = crew * blk
        for r in range(len(CHAIN)):
            cols = slice(r * deep, (r + 1) * deep)
            acc[cols, :] = contract_first(x_all[:, cols], d).astype(BF)
        for j in range(DEVS):
            row = (j % crew) * blk
            at_row = pl.multiple_of(scalars[2 * DEVS + j] * blk, blk)
            gg_refs[j // crew][row : row + blk, :] = acc[pl.ds(at_row, blk), :]


def rows_grad_kernel(scalars, d_ref, *refs, counts):
    groups, refs = grouped(refs, counts)
    gx_refs, (w_all, sems) = refs[:2], refs[2:]

    @pl.when(pl.program_id(0) == 0)
    def _():
        place_weights(scalars, groups, w_all, sems, lambda copy: copy.start())
        place_weights(scalars, groups, w_all, sems, lambda copy: copy.wait())

    store_rows_grad(scalars[DEVS], contract_last(d_ref[...], w_all[...]), gx_refs, None)


def second_kernel(scalars, mine_ref, other_ref, cot_ref, *refs, counts):
    groups, refs = grouped(refs, counts)
    prev, gx_refs, (d_ref, w_all, x_tile, sems) = refs[:2], refs[2:4], refs[4:]
    step = pl.program_id(0)
    ck = d_ref.shape[1]

    @pl.when(step == 0)
    def _():
        place_weights(scalars, groups, w_all, sems, lambda copy: copy.start())

    place_rows(scalars[DEVS], x_tile, mine_ref, other_ref)

    @pl.when(step == 0)
    def _():
        place_weights(scalars, groups, w_all, sems, lambda copy: copy.wait())

    d_gate, d_up = front(x_tile[...], w_all, cot_ref[0, :, :ck], cot_ref[0, :, ck:])
    d_ref[...] = d_gate
    gx = contract_last(jnp.concatenate([d_gate, d_up], axis=1), w_all[...])
    store_rows_grad(scalars[DEVS], gx, gx_refs, prev)


def gate_grad_kernel(scalars, mine_ref, other_ref, d_ref, *refs):
    out_refs, (x_all, acc) = refs[: len(CHAIN)], refs[len(CHAIN) :]
    step = pl.program_id(0)
    core = scalars[DEVS]
    crew = len(CREW)
    for s in range(crew):
        tile = x_all.at[s * TILE : (s + 1) * TILE]
        place_rows(core, tile, mine_ref.at[s : s + 1], other_ref.at[s : s + 1])
    deep = x_all.shape[1]
    here = pl.ds(pl.multiple_of(step * deep, deep), deep)
    acc[here, :] = contract_first(x_all[...], d_ref[...]).astype(BF)

    @pl.when(step == pl.num_programs(0) - 1)
    def _():
        blk = deep // crew
        for j in range(DEVS):
            row = (j % crew) * blk
            at_row = pl.multiple_of(scalars[j] * blk, blk)
            out_refs[j // crew][row : row + blk, :] = acc[pl.ds(at_row, blk), :]


def kernel_call(body, name, scalars, operands, in_specs, out_specs, out_shape, scratch, flops, limit):
    return pl.pallas_call(
        body,
        grid_spec=pltpu.PrefetchScalarGridSpec(
            num_scalar_prefetch=1,
            grid=(len(CREW),),
            in_specs=in_specs,
            out_specs=out_specs,
            scratch_shapes=scratch,
        ),
        out_shape=out_shape,
        compiler_params=pltpu.CompilerParams(vmem_limit_bytes=limit * 1024 * 1024),
        cost_estimate=pl.CostEstimate(flops=flops, bytes_accessed=2**23, transcendentals=0),
        name=name,
    )(scalars, *operands)


def spec_of_cols(wide, col):
    return pl.BlockSpec((1, TILE // 2, wide), lambda i, o: (i, 0, col))


def flat_of(groups):
    counts = [(g[0].shape[0], len(g)) for g in groups]
    return counts, [v for g in groups for v in g]


def first_chunk(scalars, mine, other, groups, width, ck, cot_col):
    counts, flat = flat_of(groups)
    rows = len(CREW) * TILE
    deep = width // len(CHAIN)
    d, *parts = kernel_call(
        lambda *a: first_kernel(*a, counts=counts),
        "first_chunk",
        scalars,
        [mine, other, mine, mine] + flat,
        [
            spec_of_cols(width, 0),
            spec_of_cols(width, 0),
            spec_of_cols(ck, cot_col // ck),
            spec_of_cols(ck, cot_col // ck + 1),
        ]
        + [pl.BlockSpec(memory_space=pltpu.HBM)] * len(flat),
        [pl.BlockSpec((TILE, 2 * ck), lambda i, o: (i, 0))]
        + [pl.BlockSpec((deep, ck), lambda i, o: (0, 0))] * len(CHAIN),
        [jax.ShapeDtypeStruct((rows, 2 * ck), BF)]
        + [jax.ShapeDtypeStruct((deep, ck), BF)] * len(CHAIN),
        [
            pltpu.VMEM((width, 2 * ck), BF),
            pltpu.VMEM((rows, width), BF),
            pltpu.VMEM((rows, ck), BF),
            pltpu.VMEM((width, ck), BF),
            pltpu.SemaphoreType.DMA((DEVS,)),
        ],
        6 * rows * width * ck,
        32,
    )
    return d, parts


def rows_grad(scalars, d, groups, width):
    counts, flat = flat_of(groups)
    rows, wide = d.shape
    gx_spec = pl.BlockSpec((TILE, width // 2), lambda i, o: (i, 0))
    return kernel_call(
        lambda *a: rows_grad_kernel(*a, counts=counts),
        "rows_grad",
        scalars,
        [d] + flat,
        [pl.BlockSpec((TILE, wide), lambda i, o: (i, 0))]
        + [pl.BlockSpec(memory_space=pltpu.HBM)] * len(flat),
        [gx_spec] * 2,
        [jax.ShapeDtypeStruct((rows, width // 2), BF)] * 2,
        [pltpu.VMEM((width, wide), BF), pltpu.SemaphoreType.DMA((DEVS,))],
        2 * rows * width * wide,
        24,
    )


def second_chunk(scalars, mine, other, groups, prev, width, ck, cot_col):
    counts, flat = flat_of(groups)
    rows = len(CREW) * TILE
    gx_spec = pl.BlockSpec((TILE, width // 2), lambda i, o: (i, 0))
    return kernel_call(
        lambda *a: second_kernel(*a, counts=counts),
        "second_chunk",
        scalars,
        [mine, other, mine] + flat + list(prev),
        [
            spec_of_cols(width, 0),
            spec_of_cols(width, 0),
            spec_of_cols(2 * ck, cot_col // (2 * ck)),
        ]
        + [pl.BlockSpec(memory_space=pltpu.HBM)] * len(flat)
        + [gx_spec] * 2,
        [gx_spec] * 2 + [pl.BlockSpec((TILE, ck), lambda i, o: (i, 0))],
        [jax.ShapeDtypeStruct((rows, width // 2), BF)] * 2
        + [jax.ShapeDtypeStruct((rows, ck), BF)],
        [
            pltpu.VMEM((width, 2 * ck), BF),
            pltpu.VMEM((TILE, width), BF),
            pltpu.SemaphoreType.DMA((DEVS,)),
        ],
        8 * rows * width * ck,
        24,
    )


def gate_grad(scalars, mine, other, d, width):
    rows, ck = d.shape
    steps = len(CREW)
    deep = width // steps
    x_spec = pl.BlockSpec((steps, TILE // 2, width // steps), lambda i, o: (0, 0, i))
    return kernel_call(
        gate_grad_kernel,
        "gate_grad",
        scalars,
        [mine, other, d],
        [x_spec, x_spec, pl.BlockSpec((rows, ck), lambda i, o: (0, 0))],
        [pl.BlockSpec((deep, ck), lambda i, o: (0, 0))] * len(CHAIN),
        [jax.ShapeDtypeStruct((deep, ck), BF)] * len(CHAIN),
        [pltpu.VMEM((rows, deep), BF), pltpu.VMEM((width, ck), BF)],
        2 * rows * width * ck,
        24,
    )


def join_kernel(scalars, *refs, quarter):
    out = refs[-1]
    for i, ref in enumerate(refs[:-1]):
        ck = ref.shape[1]
        start = scalars[DEVS + 2 + i % len(CREW)] * quarter
        if i >= len(CREW):
            start = start + refs[0].shape[1]
        out[:, pl.ds(pl.multiple_of(start, 128), ck)] = ref[...].astype(F32)


def join_call(scalars, pieces):
    depth = pieces[0].shape[0]
    quarter = pieces[0].shape[1] + pieces[-1].shape[1]
    vmem = pl.BlockSpec(memory_space=pltpu.VMEM)
    return pl.pallas_call(
        lambda *a: join_kernel(*a, quarter=quarter),
        in_specs=[pl.BlockSpec(memory_space=pltpu.SMEM)] + [vmem] * len(pieces),
        out_specs=vmem,
        out_shape=jax.ShapeDtypeStruct((depth, len(CREW) * quarter), F32),
        compiler_params=pltpu.CompilerParams(vmem_limit_bytes=16 * 1024 * 1024),
        name="join_quarters",
    )(scalars, *pieces)


def split_plan(x_in, cotangent, w_gate, w_up, send_counts, recv_counts):
    rows, width = x_in.shape
    depth, hidden = w_gate.shape
    crew = len(CREW)
    quarter = hidden // crew
    core = lax.axis_index("mp")
    index = lax.axis_index("dp")
    z, place = index // crew, index % crew
    places = [place ^ m for m in CREW]
    chunks = [640, 256]
    swap = [(0, 1), (1, 0)]

    order = [z, z ^ 1, jnp.where(z < 2, 2, 1), jnp.where(z < 2, 3, 0)]
    inner = ((z == 1) | (z == 2)).astype(jnp.int32)
    scalars = [index ^ c ^ m for c in CHAIN for m in CREW] + [core, inner] + places
    scalars += [0] * (2 * DEVS - len(scalars)) + [p * crew + q for p in order for q in places]
    scalars = jnp.stack([jnp.asarray(v, jnp.int32) for v in scalars])

    first = pieces_of_first(scalars, w_gate, w_up, chunks[0], quarter)
    own = first[0]
    own_far = send(own, FAR)
    own_near = send(own, NEAR)
    rest = crew_swap(first)[1:]
    own_near, x_in, cotangent = tie(own_near, x_in, cotangent)
    parcels = pack_parcels(
        scalars, send_counts, recv_counts, x_in, cotangent, w_gate, w_up, chunks
    )
    rest = jnp.concatenate(rest, axis=0)
    rest, own_far, *parcels = tie(rest, own_far, *parcels)

    own_both = send(own_far, NEAR)
    rest_far = send(rest, FAR)
    rest_near = send(rest, NEAR)
    parcels = crew_swap(parcels)
    rest_far, rest_near, own_both, *parcels = tie(rest_far, rest_near, own_both, *parcels)

    rest_both = send(rest_far, NEAR)
    mine = jnp.stack(parcels)
    other = lax.ppermute(mine, "mp", swap)
    second = mine[:, :, width + 2 * quarter :].reshape(crew * depth, 2 * chunks[1])
    rest_both, other, second = tie(rest_both, other, second)

    cot_second = width
    cot_first = width + 2 * chunks[1]

    second_near = send(second, NEAR)
    second_far = send(second, FAR)
    groups = [(own, own_near, own_far, own_both), (rest, rest_near, rest_far, rest_both)]
    d_first, parts = first_chunk(scalars, mine, other, groups, width, chunks[0], cot_first)
    second_near, second_far, d_first = tie(second_near, second_far, d_first)
    p0, p1, p2, p3 = parts

    middle = along(second, INNER)
    ends = along(second_far, TO_ENDS)
    r1 = along(p3, FROM_ENDS)
    gx = rows_grad(scalars, d_first, groups, width)
    r1, middle, ends, p2, p3, *gx = tie(r1, middle, ends, p2, p3, *gx)
    r2b = along(p2, FROM_ENDS)
    r2a = along(add(p3, r1), INNER)
    keep, give, d_second = second_chunk(
        scalars, mine, other, [(second, second_near, second_far, middle, ends)], gx,
        width, chunks[1], cot_second,
    )
    r2a, r2b, keep, give, d_second = tie(r2a, r2b, keep, give, d_second)

    theirs = lax.ppermute(give, "mp", swap)
    q_parts = gate_grad(scalars, mine, other, d_second, width)
    theirs, *q_parts = tie(theirs, *q_parts)
    q_own, q_near, q_far, q_both = q_parts
    from_near = send(q_both, NEAR)
    r3b = along(add(p2, r2b), INNER)
    r3a = along(add(p1, r2a), OUTER)
    rows_x = crew_swap(
        [
            add(keep[s * rows : (s + 1) * rows], theirs[s * rows : (s + 1) * rows])
            for s in range(crew)
        ]
    )
    from_near, r3a, r3b = tie(from_near, r3a, r3b)
    sum_far = send(add(q_far, from_near), FAR)
    sum_near = send(q_near, NEAR)
    sums = add(p0, r3a, r3b)
    firsts = crew_swap([sums[s * depth : (s + 1) * depth] for s in range(crew)])
    sum_far, sum_near, *rows_x = tie(sum_far, sum_near, *rows_x)
    sums = add(q_own, sum_near, sum_far)
    lasts = crew_swap([sums[s * depth : (s + 1) * depth] for s in range(crew)])
    return add(*rows_x), join_call(scalars, firsts + lasts)


def solution(mesh):
    sizes = dict(mesh.shape)
    splits = sizes["dp"] == DEVS and sizes["mp"] == 2
    return jax.shard_map(
        split_plan if splits else general_plan,
        mesh=mesh,
        in_specs=(
            P("dp", None),
            P("dp", "mp"),
            P("dp", "mp"),
            P("dp", "mp"),
            P("dp", None),
            P("dp", None),
        ),
        out_specs=(P("dp", "mp"), P("dp", "mp")),
        check_vma=False,
    )
```
